256 devices in a mesh: seg: 8 (over z), tm: 32 (over y, x, core).
Axes of the slice: x: 4, y: 4, z: 8, core: 2. Of those that a mesh axis runs over, the one named last changes fastest.
Arguments:
- frames: bfloat16 [49152, 1024], P(('seg', 'tm')), parts along dimension 0, may hold values from -6 to 6
- kv_weight: bfloat16 [1024, 256], replicated
- query_weight: bfloat16 [64, 1024, 128], P('tm')
- out_weight: bfloat16 [64, 128, 1024], P('tm'), may hold values from -1.5 to 1.5
- expert_ids: int32 [49152, 4], P(('seg', 'tm')), parts along dimension 0, may hold values from 0 to 63, all different within a row; in each aligned block of 192 rows (0 to 191, 192 to 383, ...) at most 24 rows name the same one
- gate_values: float32 [49152, 4], P(('seg', 'tm')), parts along dimension 0, may hold values from 0.1 to 0.6
Outputs:
- mixed: bfloat16 [49152, 1024], P(('seg', 'tm')), parts along dimension 0
The draws below stay inside these ranges and needn't reach their ends.
There are 8 independent parts, one for each index of `seg`. The reference program is written for one: setup_inputs(seed, part) draws one part's arguments, and reference() takes and returns one part's arrays. A program takes and returns all parts, laid end to end along the dimension named above; an argument that names none is the same for every part. Nothing has to cross between parts.
Inputs may be any that keep to these rules, and one draw needn't show every extreme that they name: `expert_ids`: each row names 4 different experts; within the 192 rows of one device no expert is named more than 24 times, and 24 is reached.
All inputs are finite; a program needn't handle non-finite values.
Results may differ from the reference program's by a relative error of at most 0.011.
Values may be sent and summed in bfloat16 or wider, within the bound.
A program may use at most 64 MiB of HBM per device.

```python
import math
import jax
import jax.numpy as jnp
import numpy as np
from jax import lax

D = 1024
HD = 128
TOP = 4
TOK_DEV = 192
EXPERTS = 64
LENGTH = 6144
CAP = 24
N_TM = 32


def shared_keys(key):
    return jax.random.truncated_normal(key, -6.0, 6.0, (D, HD), jnp.float32) / math.sqrt(D)


def draw_kv_weight(key, part):
    key_part = shared_keys(key)
    key = jax.random.fold_in(key, 5)
    value_part = jax.random.truncated_normal(key, -6.0, 6.0, (D, HD), jnp.float32) / math.sqrt(D)
    return jnp.concatenate([key_part, value_part], axis=1).astype(jnp.bfloat16)


def draw_query_weight(key, part):
    key = jax.random.fold_in(key, 7)
    second_key = jax.random.fold_in(key, 1)
    drawn = jax.random.truncated_normal(second_key, -6.0, 6.0, (EXPERTS, D, HD), jnp.float32)
    return (2.5 * drawn / math.sqrt(D)).astype(jnp.bfloat16)


def draw_frames(key, part):
    key = jax.random.fold_in(key, 3)
    first_key = jax.random.fold_in(key, 0)
    return jax.random.truncated_normal(first_key, -6.0, 6.0, (LENGTH, D), jnp.float32).astype(jnp.bfloat16)


def steps_of(own_key, dims, cuts, smallest, top_value):
    factor_of = 1.0
    for axis_at, blocks in cuts:
        steps = jax.random.uniform(jax.random.fold_in(jax.random.fold_in(own_key, 6), axis_at), (blocks,), jnp.float32, smallest / len(cuts), top_value / len(cuts))
        factor_of = factor_of * jnp.repeat(jnp.exp(steps), dims[axis_at] // blocks).reshape((-1,) + (1,) * (len(dims) - 1 - axis_at))
    return factor_of


def deal_out(rng, own, number, rows, number_of, top, most, slope):
    sequence = jax.random.permutation(rng, number_of)
    heavy_load, usual = shares(number_of, rows * top, most, slope, True), shares(number_of, rows * top, most, slope, False)
    places = jnp.arange(number_of)

    def named(sizes, offset_by):
        used = int((sizes > 0).sum())
        fixed = max(1, used // 4)
        shifted = fixed + (places - fixed + offset_by * (used - fixed)) % max(1, number_of - fixed)
        return jnp.zeros((number_of,), jnp.int32).at[sequence[jnp.where(places < fixed, places, shifted)]].set(jnp.asarray(sizes, jnp.int32))

    sizes = jnp.where(number % 4 == 0, named(heavy_load, number // 4), named(usual, number - number // 4 - 1))
    mixed = jax.random.permutation(jax.random.fold_in(own, 3), number_of)
    donor, sink = mixed[0:number_of // 2 * 2:2], mixed[1:number_of // 2 * 2:2]
    slack = jnp.minimum(sizes[donor] - 1, most - sizes[sink]) // 2
    slack = jnp.where((donor == sequence[0]) | (sink == sequence[0]) | (sizes[sink] == 0), 0, jnp.maximum(slack, 0))
    shifted = jax.random.randint(jax.random.fold_in(own, 4), (number_of // 2,), 0, 1 << 20) % (slack + 1)
    sizes = sizes.at[donor].add(-shifted).at[sink].add(shifted)
    labels = jnp.searchsorted(jnp.cumsum(sizes), jnp.arange(rows * top), side="right").astype(jnp.int32)
    listing = labels.reshape(top, rows).T
    listing = listing[jax.random.permutation(jax.random.fold_in(own, 1), rows)]
    offset_by = jax.random.randint(jax.random.fold_in(own, 2), (rows, 1), 0, top)
    return jnp.take_along_axis(listing, (jnp.arange(top)[None, :] + offset_by) % top, axis=1)


def shares(count, total, limit, skew, full):
    weights = [(1 << 20) // math.isqrt(grade ** skew) + 1 for grade in range(1, count + 1)]
    largest = limit if full else min(limit, max(-(-total // count), total * weights[0] // sum(weights)))
    least = 1 if total - largest >= count - 1 else 0
    given, surplus = [largest] + [least] * (count - 1), total - largest - least * (count - 1)
    while surplus > 0:
        movable = [i for i in range(1, count) if given[i] < largest] or [i for i in range(1, count) if given[i] < limit]
        pool, remaining = sum([weights[i] for i in movable]), surplus
        for i in movable:
            more = min(limit - given[i], max(1, remaining * weights[i] // pool), surplus)
            given[i] = given[i] + more
            surplus = surplus - more
    return np.array(given)


def centred(rng, dims, deviation, most, cuts=(), dtype=jnp.bfloat16):
    entries = jax.random.normal(rng, dims, jnp.float32) * deviation
    if len(cuts) > 0:
        entries = steps_of(rng, dims, cuts, -0.22, 0.18) * entries
    return jnp.clip(entries, min=-most, max=most).astype(dtype)


def setup_inputs(seed: int = 0, part: int = 0) -> dict:
    key_list = jax.random.split(jax.random.key(seed), 7)
    part_splits = jax.random.split(jax.random.fold_in(key_list[6], part), 7)
    frames = draw_frames(jax.random.fold_in(jax.random.fold_in(key_list[6], part), 71), part)
    kv_weight = draw_kv_weight(jax.random.fold_in(key_list[6], 71), part)
    query_weight = draw_query_weight(jax.random.fold_in(key_list[6], 71), part)
    out_weight = centred(key_list[3], (EXPERTS, HD, D), (HD // 8) ** -0.5, 1.5, ((0, 32),))
    expert_ids_keys = jax.random.split(jax.random.fold_in(part_splits[4], 1), LENGTH // TOK_DEV)
    expert_ids_turns = jax.random.permutation(jax.random.fold_in(part_splits[4], 3), LENGTH // TOK_DEV)
    expert_ids = jax.vmap(lambda own, number: deal_out(jax.random.fold_in(part_splits[4], 2), own, number, TOK_DEV, EXPERTS, TOP, CAP, 2))(expert_ids_keys, expert_ids_turns).reshape((LENGTH, TOP))
    gate_values = jnp.clip(0.1 + 0.5 * jax.random.uniform(part_splits[5], (LENGTH, TOP), jnp.float32) ** steps_of(part_splits[5], (LENGTH, TOP), ((0, 32),), -0.2, 0.2), 0.1, 0.6)
    return dict(frames=frames, kv_weight=kv_weight, query_weight=query_weight, out_weight=out_weight, expert_ids=expert_ids, gate_values=gate_values)


def attend(queries, key_rows, value_rows):
    scale_factor = 1.0 / math.sqrt(HD)
    scores = jnp.dot(queries, key_rows.T, preferred_element_type=jnp.float32) * scale_factor
    peak = lax.optimization_barrier(jnp.max(scores, axis=1, keepdims=True))
    exponent = jnp.exp(scores - peak)
    totals = lax.optimization_barrier(jnp.sum(exponent, axis=1, keepdims=True))
    weights = exponent.astype(jnp.bfloat16)
    summed = jnp.dot(weights, value_rows, preferred_element_type=jnp.float32)
    return (summed / totals).astype(jnp.bfloat16)

def reference(frames, kv_weight, query_weight, out_weight, expert_ids, gate_values):
    key_values = jnp.dot(frames, kv_weight, preferred_element_type=jnp.float32).astype(jnp.bfloat16)
    key_rows = key_values[:, :HD]
    value_rows = key_values[:, HD:]
    row_limit = N_TM * CAP

    def per_expert(running, expert):
        hit = expert_ids == expert
        gate_sum = lax.optimization_barrier(jnp.sum(jnp.where(hit, gate_values, jnp.zeros_like(gate_values)), axis=1))
        used = jnp.any(hit, axis=1)
        chosen = jnp.nonzero(used, size=row_limit, fill_value=0)[0].astype(jnp.int32)
        valid = jnp.arange(row_limit) < jnp.sum(used.astype(jnp.int32))
        queries = jnp.dot(frames[chosen], query_weight[expert], preferred_element_type=jnp.float32).astype(jnp.bfloat16)
        heads = attend(queries, key_rows, value_rows)
        projected = jnp.dot(heads, out_weight[expert], preferred_element_type=jnp.float32).astype(jnp.bfloat16)
        weight_rows = jnp.where(valid, gate_sum[chosen], jnp.zeros_like(gate_sum[chosen]))
        contrib = projected.astype(jnp.float32) * weight_rows[:, None]
        return (running.at[chosen].add(contrib), None)
    start_sum = jnp.zeros((LENGTH, D), jnp.float32)
    running, _ = lax.scan(per_expert, start_sum, jnp.arange(EXPERTS).astype(jnp.int32))
    return running.astype(jnp.bfloat16)
```

```python
import functools
import math

import jax
import jax.numpy as jnp
from jax import lax
from jax.experimental import pallas as pl
from jax.experimental.pallas import tpu as pltpu
from jax.sharding import PartitionSpec as P

MESH = pl.DeviceIdType.MESH
TOK = 192
D = 1024
HD = 128
CAP = 24
NEXP = 16
SLOTS = NEXP * CAP
KEYS = 6144
N_SEM = 160
BF = jnp.bfloat16
F32 = jnp.float32


def dot(a, b):
    return jnp.dot(a, b, preferred_element_type=F32)


def dot_nt(a, b):
    return lax.dot_general(a, b, (((1,), (1,)), ((), ())), preferred_element_type=F32)


def dot_tn(a, b, precision=None):
    return lax.dot_general(
        a, b, (((0,), (0,)), ((), ())), preferred_element_type=F32, precision=precision
    )


def iota(shape, dim):
    return lax.broadcasted_iota(jnp.int32, shape, dim)


def kernel(
    frames, kvw, qw, ow, ids, gates, out,
    F, R, KV, QW, OW, X, Q, VT, HDS, H, S, GS, PS, RB, send_sem, recv_sem,
):
    z = lax.axis_index("seg")
    t = lax.axis_index("tm")
    c = lax.rem(t, 2)
    x = lax.rem(t // 2, 4)
    y = t // 8

    def dev(dx=0, dy=0, dz=0, dc=0):
        yy = lax.rem(y + dy, 4)
        xx = lax.rem(x + dx, 4)
        return (lax.rem(z + dz, 8), (yy * 4 + xx) * 2 + lax.rem(c + dc, 2))

    sib = dev(dc=1)
    partners = (
        [dev(dx=d) for d in (1, 2, 3)]
        + [dev(dy=d) for d in (1, 2, 3)]
        + [dev(dz=d) for d in (1, 2, 6, 7)]
        + [sib]
    )
    barrier = pltpu.get_barrier_semaphore()
    for p in partners:
        pl.semaphore_signal(barrier, inc=1, device_id=p, device_id_type=MESH)
    pl.semaphore_wait(barrier, len(partners))

    started = []

    def send(src, dst, target):
        n = len(started)
        cp = pltpu.make_async_remote_copy(
            src_ref=src, dst_ref=dst, send_sem=send_sem.at[n], recv_sem=recv_sem.at[n],
            device_id=target, device_id_type=MESH,
        )
        cp.start()
        started.append(cp)
        return cp

    order = (1, 3, 2)
    cp_f = {}
    for d in order:
        cp_f[d] = send(frames, F.at[d], dev(dx=d))
    s4 = lax.rem(z, 4) * 512
    cp_qy = {}
    for d in order:
        cp_qy[d] = send(qw.at[pl.ds(s4, 512)], QW.at[d, pl.ds(s4, 512)], dev(dy=d))
    cp_qs = {0: send(qw, QW.at[4], sib)}

    eye = (iota((TOK, TOK), 0) == iota((TOK, TOK), 1)).astype(F32)
    route = jnp.concatenate([ids[...].astype(F32), gates[...]], axis=1)
    R[0] = dot_tn(route, eye, lax.Precision.HIGHEST)
    cp_r = {d: send(R.at[0], R.at[d], dev(dx=d)) for d in order}

    F[0] = frames[...]
    QW[0] = qw[...]
    OW[0] = ow[...]
    cp_kv = {}
    cp_ks = {}

    def key_values(d):
        rows = pl.ds(d * TOK, TOK)
        KV[rows, :] = dot(F[d], kvw[...]).astype(BF)
        for e in order:
            cp_kv[e, d] = send(KV.at[rows], KV.at[pl.ds((e * 4 + d) * TOK, TOK)], dev(dy=e))
        cp_ks[0, d] = send(KV.at[rows], KV.at[pl.ds((16 + d) * TOK, TOK)], sib)

    key_values(0)

    i16 = iota((NEXP, 1), 0)
    owner = i16 >> 1
    oc = (c + (owner >> 2)) & 1
    oy = (y - (owner & 3)) & 3
    eid = (((oy * 4 + x) * 2 + oc) * 2 + (i16 & 1)).astype(F32)
    ej, ee = iota((SLOTS, NEXP), 0), iota((SLOTS, NEXP), 1) * CAP
    expand = (ej >= ee) & (ej < ee + CAP)
    e_rows = expand.astype(F32).astype(BF)
    i_col = jnp.sum(jnp.where(expand, ej - ee, 0).astype(F32), axis=1, keepdims=True)
    tj, te = iota((NEXP, SLOTS), 1), iota((NEXP, SLOTS), 0) * CAP
    e_cols = ((tj >= te) & (tj < te + CAP)).astype(F32)
    earlier = (iota((TOK, TOK), 0) < iota((TOK, TOK), 1)).astype(F32).astype(BF)

    def select(d):
        r = R[d]
        hit = jnp.zeros((NEXP, TOK), F32)
        gate = jnp.zeros((NEXP, TOK), F32)
        for k in range(4):
            same = r[k:k + 1, :] == eid
            hit = hit + same.astype(F32)
            gate = gate + jnp.where(same, r[4 + k:5 + k, :], 0.0)
        pos = dot(hit.astype(BF), earlier)
        posm = jnp.where(hit > 0.0, pos, -1.0)
        one_hot = (dot(e_rows, posm.astype(BF)) == i_col).astype(F32)
        S[d] = one_hot.astype(BF)
        gate_rows = jnp.dot(
            e_rows.astype(F32), gate, preferred_element_type=F32, precision=lax.Precision.HIGHEST
        )
        GS[pl.ds(d * SLOTS, SLOTS), :] = jnp.broadcast_to(
            jnp.sum(one_hot * gate_rows, axis=1, keepdims=True), (SLOTS, HD)
        )
        picked = dot(S[d], F[d]).astype(BF)
        for p in range(8):
            X[p, d * 48:(d + 1) * 48, :] = picked[p * 48:(p + 1) * 48, :]

    select(0)

    cp_qz = {}
    for e in order:
        cp_qy[e].wait_recv()
        mine = QW.at[e, pl.ds(s4, 512)]
        lo, hi = QW.at[e, pl.ds(s4, 256)], QW.at[e, pl.ds(s4 + 256, 256)]
        cp_qz[e] = [
            send(mine, mine, dev(dz=1)), send(mine, mine, dev(dz=7)),
            send(lo, lo, dev(dz=2)), send(hi, hi, dev(dz=6)),
        ]

    def from_y(e, d):
        cp_kv[e, d].wait_recv()
        rows = pl.ds((e * 4 + d) * TOK, TOK)
        cp_ks[e, d] = send(KV.at[rows], KV.at[pl.ds((16 + e * 4 + d) * TOK, TOK)], sib)

    for d in order:
        cp_f[d].wait_recv()
        key_values(d)
        cp_r[d].wait_recv()
        select(d)

    s2 = lax.rem(z, 2) * 128
    cp_oy = {}
    for e in order:
        cp_oy[e] = send(ow.at[pl.ds(s2, 128)], OW.at[e, pl.ds(s2, 128)], dev(dy=e))
    cp_os = {0: send(ow, OW.at[4], sib)}

    for e in order:
        for d in (0,) + order:
            from_y(e, d)

    row = iota((TOK, 1), 0)
    first = jnp.zeros((TOK, 1), jnp.bool_)
    for b in range(4):
        first = first | ((row >= b * 48) & (row < b * 48 + CAP))

    def project_q(p):
        w = jnp.concatenate([QW[p, 0:D, :], QW[p, D:2 * D, :]], axis=1)
        both = dot(X[p], w)
        q = jnp.where(first, both[:, :HD], both[:, HD:]).astype(BF)
        for b in range(4):
            Q[b * SLOTS + p * 48:b * SLOTS + (p + 1) * 48, :] = q[b * 48:(b + 1) * 48, :]

    project_q(0)
    for e in order:
        for cp in cp_qz[e]:
            cp.wait_recv()
        cp_qs[e] = send(QW.at[e], QW.at[4 + e], sib)
        project_q(e)
    for e in (0,) + order:
        cp_qs[e].wait_recv()
        project_q(4 + e)
    for cp in cp_ks.values():
        cp.wait_recv()

    VT[HD:HD + 16, :] = jnp.ones((16, KEYS), BF)
    CH = 512
    for i in range(KEYS // CH):
        VT[:HD, i * CH:(i + 1) * CH] = KV[i * CH:(i + 1) * CH, HD:].astype(F32).T.astype(BF)

    scale = math.log2(math.e) / math.sqrt(HD)
    RW = 768

    def attend(i):
        base = i * RW
        q = Q[base:base + RW, :]
        m = None
        acc = None
        later = dot_nt(KV[0:CH, :HD], q)
        for n in range(KEYS // CH):
            s = later
            if (n + 1) * CH < KEYS:
                later = dot_nt(KV[(n + 1) * CH:(n + 2) * CH, :HD], q)
            top = jnp.max(s, axis=0, keepdims=True)
            new = top if m is None else jnp.maximum(m, top)
            p = jnp.exp2((s - new) * scale).astype(BF)
            pv = dot(VT[:, n * CH:(n + 1) * CH], p)
            acc = pv if acc is None else acc * jnp.exp2((m - new) * scale) + pv
            m = new
        heads = (acc[:HD] / acc[HD:HD + 1]).T
        HDS[base:base + RW, :] = (heads * GS[base:base + RW, :]).astype(BF)

    attend(0)
    cp_oz = {}
    for e in order:
        cp_oy[e].wait_recv()
        lo, hi = OW.at[e, pl.ds(s2, 64)], OW.at[e, pl.ds(s2 + 64, 64)]
        cp_oz[e] = [send(lo, lo, dev(dz=1)), send(hi, hi, dev(dz=7))]
    attend(1)
    for e in order:
        for cp in cp_oz[e]:
            cp.wait_recv()
        cp_os[e] = send(OW.at[e], OW.at[4 + e], sib)
    for e in (0,) + order:
        cp_os[e].wait_recv()

    half = iota((48, 1), 0) < CAP

    def project_out(b):
        for p in range(8):
            h = HDS[b * SLOTS + p * 48:b * SLOTS + (p + 1) * 48, :].astype(F32)
            pair = jnp.concatenate([jnp.where(half, h, 0.0), jnp.where(half, 0.0, h)], axis=1)
            H[:, p * 256:(p + 1) * 256] = dot_tn(
                S[b, p * 48:(p + 1) * 48, :], pair.astype(BF)
            ).astype(BF)
        return dot(H[...], OW[...].reshape(2048, D))

    cp_back = {}
    for d in (2, 1, 3):
        PS[d - 1] = project_out(d).astype(BF)
        cp_back[d] = send(PS.at[d - 1], RB.at[d - 1], dev(dx=4 - d))
    total = project_out(0)
    for d in (1, 3, 2):
        cp_back[d].wait_recv()
        total = total + RB[d - 1].astype(F32)
    out[...] = total.astype(BF)
    for cp in started:
        cp.wait_send()


def on_device(frames, kv_weight, query_weight, out_weight, expert_ids, gate_values):
    vmem = pl.BlockSpec(memory_space=pltpu.VMEM)
    return pl.pallas_call(
        kernel,
        out_shape=jax.ShapeDtypeStruct((TOK, D), BF),
        in_specs=[vmem] * 6,
        out_specs=vmem,
        scratch_shapes=[
            pltpu.VMEM((4, TOK, D), BF),
            pltpu.VMEM((4, 8, TOK), F32),
            pltpu.VMEM((KEYS, 2 * HD), BF),
            pltpu.VMEM((8, 2 * D, HD), BF),
            pltpu.VMEM((8, 2 * HD, D), BF),
            pltpu.VMEM((8, TOK, D), BF),
            pltpu.VMEM((4 * SLOTS, HD), BF),
            pltpu.VMEM((HD + 16, KEYS), BF),
            pltpu.VMEM((4 * SLOTS, HD), BF),
            pltpu.VMEM((TOK, 2 * D), BF),
            pltpu.VMEM((4, SLOTS, TOK), BF),
            pltpu.VMEM((4 * SLOTS, HD), F32),
            pltpu.VMEM((3, TOK, D), BF),
            pltpu.VMEM((3, TOK, D), BF),
            pltpu.SemaphoreType.DMA((N_SEM,)),
            pltpu.SemaphoreType.DMA((N_SEM,)),
        ],
        compiler_params=pltpu.CompilerParams(
            collective_id=0, has_side_effects=True, vmem_limit_bytes=56 << 20
        ),
        cost_estimate=pl.CostEstimate(
            flops=8_000_000_000, bytes_accessed=4_000_000, transcendentals=9_500_000
        ),
        name="moh",
    )(
        frames,
        kv_weight,
        query_weight.reshape(2 * D, HD),
        out_weight.reshape(2 * HD, D),
        expert_ids,
        gate_values,
    )


def solution(mesh):
    placed = (
        P(("seg", "tm"), None),
        P(),
        P("tm", None, None),
        P("tm", None, None),
        P(("seg", "tm"), None),
        P(("seg", "tm"), None),
    )
    return jax.shard_map(
        on_device, mesh=mesh, in_specs=placed, out_specs=P(("seg", "tm"), None), check_vma=False
    )
```

```python
import functools
import math

import jax
import jax.numpy as jnp
from jax import lax
from jax.experimental import pallas as pl
from jax.experimental.pallas import tpu as pltpu
from jax.sharding import PartitionSpec as P

MESH = pl.DeviceIdType.MESH
TOK = 192
D = 1024
HD = 128
CAP = 24
NEXP = 16
SLOTS = NEXP * CAP
KEYS = 6144
N_SEM = 96
WC = 512
PLACE = (3, 1, 0, 2)
BF = jnp.bfloat16
F32 = jnp.float32


def dot(a, b):
    return jnp.dot(a, b, preferred_element_type=F32)


def dot_nt(a, b):
    return lax.dot_general(a, b, (((1,), (1,)), ((), ())), preferred_element_type=F32)


def dot_tn(a, b, precision=None):
    return lax.dot_general(
        a, b, (((0,), (0,)), ((), ())), preferred_element_type=F32, precision=precision
    )


def iota(shape, dim):
    return lax.broadcasted_iota(jnp.int32, shape, dim)


def kernel(
    frames, kvw, qw, ow, ids, gates, out,
    F, R, KV, QW, OW, X, Q, VT, HDS, H, S, GS, PS, RB, send_sem, recv_sem,
):
    z = lax.axis_index("seg")
    t = lax.axis_index("tm")
    c = lax.rem(t, 2)
    x = lax.rem(t // 2, 4)
    y = t // 8

    def dev(dx=0, dy=0, dc=0):
        yy = lax.rem(y + dy, 4)
        xx = lax.rem(x + dx, 4)
        return (z, (yy * 4 + xx) * 2 + lax.rem(c + dc, 2))

    sib = dev(dc=1)
    partners = [dev(dx=d) for d in (1, 2, 3)] + [dev(dy=d) for d in (1, 2, 3)] + [sib]
    barrier = pltpu.get_barrier_semaphore()
    for p in partners:
        pl.semaphore_signal(barrier, inc=1, device_id=p, device_id_type=MESH)
    pl.semaphore_wait(barrier, len(partners))

    started = []

    def send(src, dst, target):
        n = len(started)
        cp = pltpu.make_async_remote_copy(
            src_ref=src, dst_ref=dst, send_sem=send_sem.at[n], recv_sem=recv_sem.at[n],
            device_id=target, device_id_type=MESH,
        )
        cp.start()
        started.append(cp)
        return cp

    class Ring:
        def __init__(self, axis, own, slot, size):
            self.up, self.down = dev(**{axis: 1}), dev(**{axis: 3})
            self.slot, h = slot, size // 2
            self.a, self.b = pl.ds(0, h), pl.ds(h, h)
            a, b = own.at[self.a], own.at[self.b]
            self.a1 = send(a, slot(1).at[self.a], self.up)
            self.b3 = send(b, slot(3).at[self.b], self.down)
            self.b1 = send(b, slot(1).at[self.b], self.up)
            self.a3 = send(a, slot(3).at[self.a], self.down)

        def pass_on(self):
            self.a1.wait_recv()
            self.a2 = send(self.slot(1).at[self.a], self.slot(2).at[self.a], self.up)
            self.b3.wait_recv()
            self.b2 = send(self.slot(3).at[self.b], self.slot(2).at[self.b], self.down)

        def wait(self, d):
            for cp in {1: (self.b1,), 3: (self.a3,), 2: (self.a2, self.b2)}[d]:
                cp.wait_recv()

    def kv_at(d, e=0, n=1, sibling=False):
        return KV.at[pl.ds((16 * sibling + d * 4 + e) * TOK, n * TOK)]

    cp_ks = []

    def kv_to_sib(*block):
        cp_ks.append(send(kv_at(*block), kv_at(*block, sibling=True), sib))

    def key_values(d):
        KV[d * 4 * TOK:(d * 4 + 1) * TOK, :] = dot(F[d], kvw[...]).astype(BF)
        kv_to_sib(d)

    order = (1, 3, 2)
    ring_f = Ring("dx", frames, lambda d: F.at[d], TOK)
    R[0, 0:4] = ids[...].astype(F32)
    R[0, 4:8] = gates[...]
    cp_r = {d: send(R.at[0], R.at[d], dev(dx=d)) for d in order}
    F[0] = frames[...]
    key_values(0)
    cp_k = {e: send(kv_at(0), kv_at(0, e), dev(dy=e)) for e in order}
    ring_q = [
        Ring("dy", qw.at[pl.ds(j * D, D)], lambda e, j=j: QW.at[e, pl.ds(j * D, D)], D)
        for j in range(2)
    ]
    cp_qs = [send(qw, QW.at[4], sib)]
    QW[0] = qw[...]
    for j in range(2):
        OW[j, 0] = ow[:, j * WC:(j + 1) * WC]

    i16 = iota((NEXP, 1), 0)
    owner = i16 >> 1
    oc = (c + (owner >> 2)) & 1
    oy = (y - (owner & 3)) & 3
    eid = (((oy * 4 + x) * 2 + oc) * 2 + (i16 & 1)).astype(F32)
    ej, ee = iota((SLOTS, NEXP), 0), iota((SLOTS, NEXP), 1) * CAP
    expand = (ej >= ee) & (ej < ee + CAP)
    e_rows = expand.astype(F32).astype(BF)
    i_col = jnp.sum(jnp.where(expand, ej - ee, 0).astype(F32), axis=1, keepdims=True)
    tj, te = iota((NEXP, SLOTS), 1), iota((NEXP, SLOTS), 0) * CAP
    e_cols = ((tj >= te) & (tj < te + CAP)).astype(F32)
    earlier = (iota((TOK, TOK), 0) < iota((TOK, TOK), 1)).astype(F32).astype(BF)

    def select(d):
        r = R[d]
        hit = jnp.zeros((NEXP, TOK), F32)
        gate = jnp.zeros((NEXP, TOK), F32)
        for k in range(4):
            same = r[k:k + 1, :] == eid
            hit = hit + same.astype(F32)
            gate = gate + jnp.where(same, r[4 + k:5 + k, :], 0.0)
        pos = dot(hit.astype(BF), earlier)
        posm = jnp.where(hit > 0.0, pos, -1.0)
        one_hot = (dot(e_rows, posm.astype(BF)) == i_col).astype(F32)
        S[d] = one_hot.astype(BF)
        gate_rows = jnp.dot(
            e_rows.astype(F32), gate, preferred_element_type=F32, precision=lax.Precision.HIGHEST
        )
        GS[PLACE[d] * SLOTS:(PLACE[d] + 1) * SLOTS, :] = jnp.broadcast_to(
            jnp.sum(one_hot * gate_rows, axis=1, keepdims=True), (SLOTS, HD)
        )
        picked = dot(S[d], F[d]).astype(BF)
        for p in range(8):
            X[p, d * 48:(d + 1) * 48, :] = picked[p * 48:(p + 1) * 48, :]

    select(0)

    ring_f.pass_on()
    for e in order:
        cp_k[e].wait_recv()
    ring_kx = Ring("dx", kv_at(0, 1, 3), lambda d: kv_at(d, 1, 3), 3 * TOK)
    kv_to_sib(0, 1, 3)
    ring_q[0].pass_on()
    for d in (1, 3):
        ring_f.wait(d)
        key_values(d)
        cp_r[d].wait_recv()
        select(d)
    ring_q[1].pass_on()
    ring_o = {}
    cp_os = {}

    def out_weights(j):
        cols = pl.ds(j * WC, WC)
        ring_o[j] = Ring("dy", ow.at[:, cols], lambda e: OW.at[j, e], 2 * HD)
        cp_os[j] = [send(OW.at[j, 0], OW.at[j, 4], sib)]

    out_weights(0)
    ring_f.wait(2)
    key_values(2)
    cp_r[2].wait_recv()
    select(2)
    ring_kx.pass_on()

    row = iota((TOK, 1), 0)
    first = jnp.zeros((TOK, 1), jnp.bool_)
    for b in range(4):
        first = first | ((row >= b * 48) & (row < b * 48 + CAP))

    def project_q(p):
        w = jnp.concatenate([QW[p, 0:D, :], QW[p, D:2 * D, :]], axis=1)
        both = dot(X[p], w)
        q = jnp.where(first, both[:, :HD], both[:, HD:]).astype(BF)
        for b in range(4):
            at = PLACE[b] * SLOTS + p * 48
            Q[at:at + 48, :] = q[b * 48:(b + 1) * 48, :]

    project_q(0)
    for e in (1, 3):
        for ring in ring_q:
            ring.wait(e)
        cp_qs.append(send(QW.at[e], QW.at[4 + e], sib))
        project_q(e)
    for d in (1, 3):
        ring_kx.wait(d)
        kv_to_sib(d, 1, 3)
    for ring in ring_q:
        ring.wait(2)
    cp_qs.append(send(QW.at[2], QW.at[6], sib))
    ring_kx.wait(2)
    kv_to_sib(2, 1, 3)
    project_q(2)
    for e, cp in zip((0,) + order, cp_qs):
        cp.wait_recv()
        project_q(4 + e)
    for cp in cp_ks:
        cp.wait_recv()

    VT[HD:HD + 16, :] = jnp.ones((16, KEYS), BF)
    CH = 512
    for i in range(KEYS // CH):
        VT[:HD, i * CH:(i + 1) * CH] = KV[i * CH:(i + 1) * CH, HD:].astype(F32).T.astype(BF)

    scale = math.log2(math.e) / math.sqrt(HD)
    RW = 768

    def attend(i, between=None):
        base = i * RW
        q = Q[base:base + RW, :]
        m = None
        acc = None
        later = dot_nt(KV[0:CH, :HD], q)
        for n in range(KEYS // CH):
            s = later
            if between is not None and n in between:
                between[n]()
            if (n + 1) * CH < KEYS:
                later = dot_nt(KV[(n + 1) * CH:(n + 2) * CH, :HD], q)
            top = jnp.max(s, axis=0, keepdims=True)
            new = top if m is None else jnp.maximum(m, top)
            p = jnp.exp2((s - new) * scale).astype(BF)
            pv = dot(VT[:, n * CH:(n + 1) * CH], p)
            acc = pv if acc is None else acc * jnp.exp2((m - new) * scale) + pv
            m = new
        heads = (acc[:HD] / acc[HD:HD + 1]).T
        HDS[base:base + RW, :] = (heads * GS[base:base + RW, :]).astype(BF)

    def next_weights():
        ring_o[0].pass_on()
        out_weights(1)

    def all_weights(j):
        for e in order:
            ring_o[j].wait(e)
            cp_os[j].append(send(OW.at[j, e], OW.at[j, 4 + e], sib))
        for cp in cp_os[j]:
            cp.wait_recv()

    half = iota((48, 1), 0) < CAP

    def gather_heads(b):
        for p in range(8):
            at = PLACE[b] * SLOTS + p * 48
            h = HDS[at:at + 48, :].astype(F32)
            pair = jnp.concatenate([jnp.where(half, h, 0.0), jnp.where(half, 0.0, h)], axis=1)
            H[b, :, p * 256:(p + 1) * 256] = dot_tn(
                S[b, p * 48:(p + 1) * 48, :], pair.astype(BF)
            ).astype(BF)

    def project_out(b, j):
        return dot(H[b], OW[j].reshape(2 * D, WC))

    cp_back = {}

    def give_back(d, j):
        PS[j, d - 1] = project_out(d, j).astype(BF)
        cp_back[j, d] = send(PS.at[j, d - 1], RB.at[j, d - 1], dev(dx=4 - d))

    attend(0, {0: next_weights})
    gather_heads(2)
    gather_heads(1)
    all_weights(0)
    give_back(2, 0)
    give_back(1, 0)
    attend(1, {6: lambda: ring_o[1].pass_on()})
    gather_heads(3)
    give_back(3, 0)
    all_weights(1)
    give_back(2, 1)
    give_back(1, 1)
    give_back(3, 1)
    gather_heads(0)
    for j in range(2):
        total = project_out(0, j)
        for d in (2, 1, 3):
            cp_back[j, d].wait_recv()
            total = total + RB[j, d - 1].astype(F32)
        out[:, j * WC:(j + 1) * WC] = total.astype(BF)
    for cp in started:
        cp.wait_send()


def on_device(frames, kv_weight, query_weight, out_weight, expert_ids, gate_values):
    vmem = pl.BlockSpec(memory_space=pltpu.VMEM)
    return pl.pallas_call(
        kernel,
        out_shape=jax.ShapeDtypeStruct((TOK, D), BF),
        in_specs=[vmem] * 6,
        out_specs=vmem,
        scratch_shapes=[
            pltpu.VMEM((4, TOK, D), BF),
            pltpu.VMEM((4, 8, TOK), F32),
            pltpu.VMEM((KEYS, 2 * HD), BF),
            pltpu.VMEM((8, 2 * D, HD), BF),
            pltpu.VMEM((2, 8, 2 * HD, WC), BF),
            pltpu.VMEM((8, TOK, D), BF),
            pltpu.VMEM((4 * SLOTS, HD), BF),
            pltpu.VMEM((HD + 16, KEYS), BF),
            pltpu.VMEM((4 * SLOTS, HD), BF),
            pltpu.VMEM((4, TOK, 2 * D), BF),
            pltpu.VMEM((4, SLOTS, TOK), BF),
            pltpu.VMEM((4 * SLOTS, HD), F32),
            pltpu.VMEM((2, 3, TOK, WC), BF),
            pltpu.VMEM((2, 3, TOK, WC), BF),
            pltpu.SemaphoreType.DMA((N_SEM,)),
            pltpu.SemaphoreType.DMA((N_SEM,)),
        ],
        compiler_params=pltpu.CompilerParams(
            collective_id=0, has_side_effects=True, vmem_limit_bytes=56 << 20
        ),
        cost_estimate=pl.CostEstimate(
            flops=8_000_000_000, bytes_accessed=4_000_000, transcendentals=9_500_000
        ),
        name="moh",
    )(
        frames,
        kv_weight,
        query_weight.reshape(2 * D, HD),
        out_weight.reshape(2 * HD, D),
        expert_ids.T,
        gate_values.T,
    )


def solution(mesh):
    placed = (
        P(("seg", "tm"), None),
        P(),
        P("tm", None, None),
        P("tm", None, None),
        P(("seg", "tm"), None),
        P(("seg", "tm"), None),
    )
    return jax.shard_map(
        on_device, mesh=mesh, in_specs=placed, out_specs=P(("seg", "tm"), None), check_vma=False
    )
```

```python
import functools
import math

import jax
import jax.numpy as jnp
from jax import lax
from jax.experimental import pallas as pl
from jax.experimental.pallas import tpu as pltpu
from jax.sharding import PartitionSpec as P

MESH = pl.DeviceIdType.MESH
TOK = 192
D = 1024
HD = 128
CAP = 24
NEXP = 16
SLOTS = NEXP * CAP
KEYS = 6144
N_SEM = 128
NC = 4
WC = D // NC
RANK = (0, 2, 6, 4, 1, 3, 7, 5)
CHUNKS = (0, 4, 1, 3, 5, 7, 2, 6)
CH = 768
BF = jnp.bfloat16
F32 = jnp.float32


def dot(a, b):
    return jnp.dot(a, b, preferred_element_type=F32)


def dot_nt(a, b):
    return lax.dot_general(a, b, (((1,), (1,)), ((), ())), preferred_element_type=F32)


def dot_tn(a, b, precision=None):
    return lax.dot_general(
        a, b, (((0,), (0,)), ((), ())), preferred_element_type=F32, precision=precision
    )


def place(p, b):
    return RANK[p] * 144 + (b - 1) * 48 if b else 1152 + RANK[p] * 48


def iota(shape, dim):
    return lax.broadcasted_iota(jnp.int32, shape, dim)


def kernel(
    frames, kvw, qw, ow, ids, gates, out,
    F, R, KV, QW, OW, X, Q, VT, HDS, H, S, GS, PS, RB, send_sem, recv_sem,
):
    z = lax.axis_index("seg")
    t = lax.axis_index("tm")
    c = lax.rem(t, 2)
    x = lax.rem(t // 2, 4)
    y = t // 8

    def dev(dx=0, dy=0, dc=0):
        yy = lax.rem(y + dy, 4)
        xx = lax.rem(x + dx, 4)
        return (z, (yy * 4 + xx) * 2 + lax.rem(c + dc, 2))

    sib = dev(dc=1)
    partners = [dev(dx=d) for d in (1, 2, 3)] + [dev(dy=d) for d in (1, 2, 3)] + [sib]
    barrier = pltpu.get_barrier_semaphore()
    for p in partners:
        pl.semaphore_signal(barrier, inc=1, device_id=p, device_id_type=MESH)
    pl.semaphore_wait(barrier, len(partners))

    started = []

    def send(src, dst, target):
        n = len(started)
        cp = pltpu.make_async_remote_copy(
            src_ref=src, dst_ref=dst, send_sem=send_sem.at[n], recv_sem=recv_sem.at[n],
            device_id=target, device_id_type=MESH,
        )
        cp.start()
        started.append(cp)
        return cp

    class Ring:
        def __init__(self, axis, own, slot, size):
            self.up, self.down = dev(**{axis: 1}), dev(**{axis: 3})
            self.slot, h = slot, size // 2
            self.a, self.b = pl.ds(0, h), pl.ds(h, h)
            a, b = own.at[self.a], own.at[self.b]
            self.a1 = send(a, slot(1).at[self.a], self.up)
            self.b3 = send(b, slot(3).at[self.b], self.down)
            self.b1 = send(b, slot(1).at[self.b], self.up)
            self.a3 = send(a, slot(3).at[self.a], self.down)

        def pass_on(self):
            self.a1.wait_recv()
            self.a2 = send(self.slot(1).at[self.a], self.slot(2).at[self.a], self.up)
            self.b3.wait_recv()
            self.b2 = send(self.slot(3).at[self.b], self.slot(2).at[self.b], self.down)

        def wait(self, d):
            for cp in {1: (self.b1,), 3: (self.a3,), 2: (self.a2, self.b2)}[d]:
                cp.wait_recv()

    def kv_at(d, e=0, n=1, sibling=False):
        return KV.at[pl.ds((16 * sibling + d * 4 + e) * TOK, n * TOK)]

    cp_ks = {}

    def kv_to_sib(*block):
        cp_ks[block] = send(kv_at(*block), kv_at(*block, sibling=True), sib)

    def key_values(d):
        KV[d * 4 * TOK:(d * 4 + 1) * TOK, :] = dot(F[d], kvw[...]).astype(BF)
        kv_to_sib(d)

    order = (1, 3, 2)
    def query_ring(j):
        rows = pl.ds(j * D, D)
        return Ring("dy", qw.at[rows], lambda e: QW.at[e, rows], D)

    ring_f = Ring("dx", frames, lambda d: F.at[d], TOK)
    ring_q = [query_ring(0)]
    R[0, 0:4] = ids[...].astype(F32)
    R[0, 4:8] = gates[...]
    cp_r = {d: send(R.at[0], R.at[d], dev(dx=d)) for d in order}
    F[0] = frames[...]
    key_values(0)
    cp_k = {e: send(kv_at(0), kv_at(0, e), dev(dy=e)) for e in order}
    ring_q.append(query_ring(1))
    cp_qs = [send(qw, QW.at[4], sib)]
    QW[0] = qw[...]
    for j in range(NC):
        OW[j, 0] = ow[:, j * WC:(j + 1) * WC]

    i16 = iota((NEXP, 1), 0)
    owner = i16 >> 1
    oc = (c + (owner >> 2)) & 1
    oy = (y - (owner & 3)) & 3
    eid = (((oy * 4 + x) * 2 + oc) * 2 + (i16 & 1)).astype(F32)
    ej, ee = iota((SLOTS, NEXP), 0), iota((SLOTS, NEXP), 1) * CAP
    expand = (ej >= ee) & (ej < ee + CAP)
    e_rows = expand.astype(F32).astype(BF)
    i_col = jnp.sum(jnp.where(expand, ej - ee, 0).astype(F32), axis=1, keepdims=True)
    earlier = (iota((TOK, TOK), 0) < iota((TOK, TOK), 1)).astype(F32).astype(BF)

    def select(d):
        r = R[d]
        hit = jnp.zeros((NEXP, TOK), F32)
        gate = jnp.zeros((NEXP, TOK), F32)
        for k in range(4):
            same = r[k:k + 1, :] == eid
            hit = hit + same.astype(F32)
            gate = gate + jnp.where(same, r[4 + k:5 + k, :], 0.0)
        pos = dot(hit.astype(BF), earlier)
        posm = jnp.where(hit > 0.0, pos, -1.0)
        one_hot = (dot(e_rows, posm.astype(BF)) == i_col).astype(F32)
        S[d] = one_hot.astype(BF)
        gate_rows = jnp.dot(
            e_rows.astype(F32), gate, preferred_element_type=F32, precision=lax.Precision.HIGHEST
        )
        gate_col = jnp.broadcast_to(
            jnp.sum(one_hot * gate_rows, axis=1, keepdims=True), (SLOTS, HD)
        )
        picked = dot(S[d], F[d]).astype(BF)
        for p in range(8):
            X[p, d * 48:(d + 1) * 48, :] = picked[p * 48:(p + 1) * 48, :]
            GS[place(p, d):place(p, d) + 48, :] = gate_col[p * 48:(p + 1) * 48, :]

    select(0)

    ring_q[0].pass_on()
    ring_f.pass_on()
    for d in (1, 3):
        ring_f.wait(d)
        key_values(d)
        cp_r[d].wait_recv()
        select(d)
    for e in order:
        cp_k[e].wait_recv()
    ring_kx = Ring("dx", kv_at(0, 1, 3), lambda d: kv_at(d, 1, 3), 3 * TOK)
    kv_to_sib(0, 1, 3)
    ring_q[1].pass_on()
    ring_o, cp_os = {}, {}

    def out_weights(j):
        cols = pl.ds(j * WC, WC)
        ring_o[j] = Ring("dy", ow.at[:, cols], lambda e: OW.at[j, e], 2 * HD)
        cp_os[j] = [send(OW.at[j, 0], OW.at[j, 4], sib)]

    def pass_weights(j):
        ring_o[j].pass_on()
        if j + 2 < NC:
            out_weights(j + 2)

    def relay_weights(j):
        for e in order:
            ring_o[j].wait(e)
            cp_os[j].append(send(OW.at[j, e], OW.at[j, 4 + e], sib))

    def have_weights(j):
        for cp in cp_os[j]:
            cp.wait_recv()

    out_weights(0)
    out_weights(1)
    ring_f.wait(2)
    key_values(2)
    cp_r[2].wait_recv()
    select(2)

    row = iota((TOK, 1), 0)
    first = jnp.zeros((TOK, 1), jnp.bool_)
    for b in range(4):
        first = first | ((row >= b * 48) & (row < b * 48 + CAP))

    def project_q(p):
        w = jnp.concatenate([QW[p, 0:D, :], QW[p, D:2 * D, :]], axis=1)
        both = dot(X[p], w)
        q = jnp.where(first, both[:, :HD], both[:, HD:]).astype(BF)
        Q[place(p, 0):place(p, 0) + 48, :] = q[:48, :]
        Q[place(p, 1):place(p, 1) + 144, :] = q[48:, :]

    project_q(0)
    cp_qs[0].wait_recv()
    project_q(4)

    cp_qn = {}

    def sib_keys(d):
        cp_ks[(d,)].wait_recv()
        cp_ks[d, 1, 3].wait_recv()

    def column_keys(d):
        ring_kx.wait(d)
        kv_to_sib(d, 1, 3)

    def relay_queries(e):
        for j in range(2):
            ring_q[j].wait(e)
            rows = pl.ds(j * D, D)
            cp_qn[e, j] = send(QW.at[e, rows], QW.at[4 + e, rows], sib)

    relay_queries(1)
    relay_queries(3)
    project_q(1)
    project_q(3)
    ring_kx.pass_on()
    for e in (1, 3):
        cp_qn[e, 0].wait_recv()
        cp_qn[e, 1].wait_recv()
        project_q(4 + e)

    VT[HD:HD + 16, :] = jnp.ones((16, KEYS), BF)
    scale = math.log2(math.e) / math.sqrt(HD)

    def attend(base, size, before):
        q = Q[base:base + size, :]

        def scores(n):
            if n in before:
                before[n]()
            keys = slice(CHUNKS[n] * CH, (CHUNKS[n] + 1) * CH)
            if base == 0:
                VT[:HD, keys] = KV[keys, HD:].astype(F32).T.astype(BF)
            return dot_nt(KV[keys, :HD], q)

        m = None
        acc = None
        later = scores(0)
        for n in range(len(CHUNKS)):
            s = later
            if n + 1 < len(CHUNKS):
                later = scores(n + 1)
            top = jnp.max(s, axis=0, keepdims=True)
            new = top if m is None else jnp.maximum(m, top)
            p = jnp.exp2((s - new) * scale).astype(BF)
            pv = dot(VT[:, CHUNKS[n] * CH:(CHUNKS[n] + 1) * CH], p)
            acc = pv if acc is None else acc * jnp.exp2((m - new) * scale) + pv
            m = new
        heads = (acc[:HD] / acc[HD:HD + 1]).T
        HDS[base:base + size, :] = (heads * GS[base:base + size, :]).astype(BF)

    half = iota((48, 1), 0) < CAP

    def gather_heads(b):
        for p in range(8):
            h = HDS[place(p, b):place(p, b) + 48, :].astype(F32)
            both = jnp.concatenate([jnp.where(half, h, 0.0), jnp.where(half, 0.0, h)], axis=1)
            H[b, :, p * 256:(p + 1) * 256] = dot_tn(
                S[b, p * 48:(p + 1) * 48, :], both.astype(BF)
            ).astype(BF)

    def project_out(b, j):
        return dot(H[b], OW[j].reshape(2 * D, WC))

    cp_back = {}

    def give_back(d, j):
        PS[j, d - 1] = project_out(d, j).astype(BF)
        cp_back[j, d] = send(PS.at[j, d - 1], RB.at[j, d - 1], dev(dx=4 - d))

    def give_all(j, *blocks):
        have_weights(j)
        for d in blocks:
            give_back(d, j)

    attend(0, 2 * SLOTS, {
        1: lambda: sib_keys(0),
        2: lambda: column_keys(1),
        3: lambda: column_keys(3),
        4: lambda: (sib_keys(1), relay_queries(2)),
        5: lambda: sib_keys(3),
        6: lambda: (column_keys(2), pass_weights(0)),
        7: lambda: sib_keys(2),
    })
    project_q(2)
    cp_qn[2, 0].wait_recv()
    cp_qn[2, 1].wait_recv()
    project_q(6)
    attend(2 * SLOTS, SLOTS, {
        1: lambda: pass_weights(1),
        6: lambda: relay_weights(0),
    })
    for d in (2, 1, 3):
        gather_heads(d)
    give_all(0, 2, 1, 3)
    attend(3 * SLOTS, SLOTS, {
        1: lambda: pass_weights(2),
        4: lambda: relay_weights(1),
        7: lambda: give_all(1, 2, 1, 3),
    })
    pass_weights(3)
    relay_weights(2)
    give_all(2, 2, 1, 3)
    relay_weights(3)
    give_all(3, 2, 1, 3)
    gather_heads(0)
    for j in range(NC):
        total = project_out(0, j)
        for d in (2, 1, 3):
            cp_back[j, d].wait_recv()
            total = total + RB[j, d - 1].astype(F32)
        out[:, j * WC:(j + 1) * WC] = total.astype(BF)
    for cp in started:
        cp.wait_send()


def on_device(frames, kv_weight, query_weight, out_weight, expert_ids, gate_values):
    vmem = pl.BlockSpec(memory_space=pltpu.VMEM)
    return pl.pallas_call(
        kernel,
        out_shape=jax.ShapeDtypeStruct((TOK, D), BF),
        in_specs=[vmem] * 6,
        out_specs=vmem,
        scratch_shapes=[
            pltpu.VMEM((4, TOK, D), BF),
            pltpu.VMEM((4, 8, TOK), F32),
            pltpu.VMEM((KEYS, 2 * HD), BF),
            pltpu.VMEM((8, 2 * D, HD), BF),
            pltpu.VMEM((NC, 8, 2 * HD, WC), BF),
            pltpu.VMEM((8, TOK, D), BF),
            pltpu.VMEM((4 * SLOTS, HD), BF),
            pltpu.VMEM((HD + 16, KEYS), BF),
            pltpu.VMEM((4 * SLOTS, HD), BF),
            pltpu.VMEM((4, TOK, 2 * D), BF),
            pltpu.VMEM((4, SLOTS, TOK), BF),
            pltpu.VMEM((4 * SLOTS, HD), F32),
            pltpu.VMEM((NC, 3, TOK, WC), BF),
            pltpu.VMEM((NC, 3, TOK, WC), BF),
            pltpu.SemaphoreType.DMA((N_SEM,)),
            pltpu.SemaphoreType.DMA((N_SEM,)),
        ],
        compiler_params=pltpu.CompilerParams(
            collective_id=0, has_side_effects=True, vmem_limit_bytes=56 << 20
        ),
        cost_estimate=pl.CostEstimate(
            flops=8_000_000_000, bytes_accessed=4_000_000, transcendentals=9_500_000
        ),
        name="moh",
    )(
        frames,
        kv_weight,
        query_weight.reshape(2 * D, HD),
        out_weight.reshape(2 * HD, D),
        expert_ids.T,
        gate_values.T,
    )


def solution(mesh):
    placed = (
        P(("seg", "tm"), None),
        P(),
        P("tm", None, None),
        P("tm", None, None),
        P(("seg", "tm"), None),
        P(("seg", "tm"), None),
    )
    return jax.shard_map(
        on_device, mesh=mesh, in_specs=placed, out_specs=P(("seg", "tm"), None), check_vma=False
    )
```

```python
import functools
import math

import jax
import jax.numpy as jnp
from jax import lax
from jax.experimental import pallas as pl
from jax.experimental.pallas import tpu as pltpu
from jax.sharding import PartitionSpec as P

MESH = pl.DeviceIdType.MESH
TOK = 192
D = 1024
HD = 128
CAP = 24
NEXP = 16
SLOTS = NEXP * CAP
KEYS = 6144
N_SEM = 128
NC = 4
WC = D // NC
RANK = (0, 2, 6, 4, 1, 3, 7, 5)
CHUNKS = (0, 4, 1, 3, 5, 7, 2, 6)
CH = 768
BF = jnp.bfloat16
F32 = jnp.float32


def dot(a, b):
    return jnp.dot(a, b, preferred_element_type=F32)


def dot_nt(a, b):
    return lax.dot_general(a, b, (((1,), (1,)), ((), ())), preferred_element_type=F32)


def dot_tn(a, b, precision=None):
    return lax.dot_general(
        a, b, (((0,), (0,)), ((), ())), preferred_element_type=F32, precision=precision
    )


def place(p, b):
    return RANK[p] * 144 + (b - 1) * 48 if b else 1152 + RANK[p] * 48


def iota(shape, dim):
    return lax.broadcasted_iota(jnp.int32, shape, dim)


def kernel(
    frames_in, kvw_in, qw_in, ow_in, ids_in, gates_in, out,
    F, R, KV, QW, OW, X, Q, VT, HDS, H, S, GS, PS, PF, TB, RB, OWN, kvw, ids, gates, send_sem, recv_sem, keep_sem,
):
    z = lax.axis_index("seg")
    t = lax.axis_index("tm")
    c = lax.rem(t, 2)
    x = lax.rem(t // 2, 4)
    y = t // 8

    def dev(dx=0, dy=0, dc=0):
        yy = lax.rem(y + dy, 4)
        xx = lax.rem(x + dx, 4)
        return (z, (yy * 4 + xx) * 2 + lax.rem(c + dc, 2))

    sib = dev(dc=1)
    partners = [dev(dx=d) for d in (1, 2, 3)] + [dev(dy=d) for d in (1, 2, 3)] + [sib]
    frames, qw, ow = F.at[0], QW.at[0], OWN
    kept = [
        pltpu.make_async_copy(src, dst, keep_sem.at[n])
        for n, (src, dst) in enumerate((
            (frames_in, frames), (kvw_in, kvw), (ids_in, ids), (gates_in, gates), (qw_in, qw), (ow_in, ow),
        ))
    ]
    for cp in kept:
        cp.start()
    barrier = pltpu.get_barrier_semaphore()
    for p in partners:
        pl.semaphore_signal(barrier, inc=1, device_id=p, device_id_type=MESH)
    pl.semaphore_wait(barrier, len(partners))

    for cp in kept:
        cp.wait()
    started = []

    def send(src, dst, target):
        n = len(started)
        cp = pltpu.make_async_remote_copy(
            src_ref=src, dst_ref=dst, send_sem=send_sem.at[n], recv_sem=recv_sem.at[n],
            device_id=target, device_id_type=MESH,
        )
        cp.start()
        started.append(cp)
        return cp

    class Ring:
        def __init__(self, axis, own, slot, size):
            self.up, self.down = dev(**{axis: 1}), dev(**{axis: 3})
            self.slot, h = slot, size // 2
            self.a, self.b = pl.ds(0, h), pl.ds(h, h)
            a, b = own.at[self.a], own.at[self.b]
            self.a1 = send(a, slot(1).at[self.a], self.up)
            self.b3 = send(b, slot(3).at[self.b], self.down)
            self.b1 = send(b, slot(1).at[self.b], self.up)
            self.a3 = send(a, slot(3).at[self.a], self.down)

        def pass_on(self):
            self.a1.wait_recv()
            self.a2 = send(self.slot(1).at[self.a], self.slot(2).at[self.a], self.up)
            self.b3.wait_recv()
            self.b2 = send(self.slot(3).at[self.b], self.slot(2).at[self.b], self.down)

        def wait(self, d):
            for cp in {1: (self.b1,), 3: (self.a3,), 2: (self.a2, self.b2)}[d]:
                cp.wait_recv()

    def kv_at(d, e=0, n=1, sibling=False):
        return KV.at[pl.ds((16 * sibling + d * 4 + e) * TOK, n * TOK)]

    cp_ks = {}

    def kv_to_sib(*block):
        cp_ks[block] = send(kv_at(*block), kv_at(*block, sibling=True), sib)

    def key_values(d):
        KV[d * 4 * TOK:(d * 4 + 1) * TOK, :] = dot(F[d], kvw[...]).astype(BF)
        kv_to_sib(d)

    order = (1, 3, 2)
    def query_ring(j):
        rows = pl.ds(j * D, D)
        return Ring("dy", qw.at[rows], lambda e: QW.at[e, rows], D)

    ring_f = Ring("dx", frames, lambda d: F.at[d], TOK)
    ring_q = [query_ring(0)]
    R[0, 0:4] = ids[...].astype(F32)
    R[0, 4:8] = gates[...]
    cp_r = {d: send(R.at[0], R.at[d], dev(dx=d)) for d in order}
    key_values(0)
    cp_k = {e: send(kv_at(0), kv_at(0, e), dev(dy=e)) for e in order}
    ring_q.append(query_ring(1))
    cp_qs = [send(qw, QW.at[4], sib)]
    for j in range(NC):
        OW[j, 0] = ow[:, j * WC:(j + 1) * WC]

    i16 = iota((NEXP, 1), 0)
    owner = i16 >> 1
    oc = (c + (owner >> 2)) & 1
    oy = (y - (owner & 3)) & 3
    eid = (((oy * 4 + x) * 2 + oc) * 2 + (i16 & 1)).astype(F32)
    ej, ee = iota((SLOTS, NEXP), 0), iota((SLOTS, NEXP), 1) * CAP
    expand = (ej >= ee) & (ej < ee + CAP)
    e_rows = expand.astype(F32).astype(BF)
    i_col = jnp.sum(jnp.where(expand, ej - ee, 0).astype(F32), axis=1, keepdims=True)
    earlier = (iota((TOK, TOK), 0) < iota((TOK, TOK), 1)).astype(F32).astype(BF)

    def select(d):
        r = R[d]
        hit = jnp.zeros((NEXP, TOK), F32)
        gate = jnp.zeros((NEXP, TOK), F32)
        for k in range(4):
            same = r[k:k + 1, :] == eid
            hit = hit + same.astype(F32)
            gate = gate + jnp.where(same, r[4 + k:5 + k, :], 0.0)
        pos = dot(hit.astype(BF), earlier)
        posm = jnp.where(hit > 0.0, pos, -1.0)
        one_hot = (dot(e_rows, posm.astype(BF)) == i_col).astype(F32)
        S[d] = one_hot.astype(BF)
        gate_rows = jnp.dot(
            e_rows.astype(F32), gate, preferred_element_type=F32, precision=lax.Precision.HIGHEST
        )
        gate_col = jnp.broadcast_to(
            jnp.sum(one_hot * gate_rows, axis=1, keepdims=True), (SLOTS, HD)
        )
        picked = dot(S[d], F[d]).astype(BF)
        for p in range(8):
            X[p, d * 48:(d + 1) * 48, :] = picked[p * 48:(p + 1) * 48, :]
            GS[place(p, d):place(p, d) + 48, :] = gate_col[p * 48:(p + 1) * 48, :]

    select(0)

    ring_q[0].pass_on()
    ring_f.pass_on()
    for d in (1, 3):
        ring_f.wait(d)
        key_values(d)
        cp_r[d].wait_recv()
        select(d)
    for e in order:
        cp_k[e].wait_recv()
    ring_kx = Ring("dx", kv_at(0, 1, 3), lambda d: kv_at(d, 1, 3), 3 * TOK)
    kv_to_sib(0, 1, 3)
    ring_q[1].pass_on()
    ring_o, cp_os = {}, {}

    def out_weights(j):
        cols = pl.ds(j * WC, WC)
        ring_o[j] = Ring("dy", ow.at[:, cols], lambda e: OW.at[j, e], 2 * HD)
        cp_os[j] = [send(OW.at[j, 0], OW.at[j, 4], sib)]

    def pass_weights(j):
        ring_o[j].pass_on()
        if j + 2 < NC:
            out_weights(j + 2)

    def relay_weights(j):
        for e in order:
            ring_o[j].wait(e)
            cp_os[j].append(send(OW.at[j, e], OW.at[j, 4 + e], sib))

    def have_weights(j):
        for cp in cp_os[j]:
            cp.wait_recv()

    out_weights(0)
    out_weights(1)
    ring_f.wait(2)
    key_values(2)
    cp_r[2].wait_recv()
    select(2)

    row = iota((TOK, 1), 0)
    first = jnp.zeros((TOK, 1), jnp.bool_)
    for b in range(4):
        first = first | ((row >= b * 48) & (row < b * 48 + CAP))

    def project_q(p):
        w = jnp.concatenate([QW[p, 0:D, :], QW[p, D:2 * D, :]], axis=1)
        both = dot(X[p], w)
        q = jnp.where(first, both[:, :HD], both[:, HD:]).astype(BF)
        Q[place(p, 0):place(p, 0) + 48, :] = q[:48, :]
        Q[place(p, 1):place(p, 1) + 144, :] = q[48:, :]

    project_q(0)
    cp_qs[0].wait_recv()
    project_q(4)

    cp_qn = {}

    def sib_keys(d):
        cp_ks[(d,)].wait_recv()
        cp_ks[d, 1, 3].wait_recv()

    def column_keys(d):
        ring_kx.wait(d)
        kv_to_sib(d, 1, 3)

    def relay_queries(e):
        for j in range(2):
            ring_q[j].wait(e)
            rows = pl.ds(j * D, D)
            cp_qn[e, j] = send(QW.at[e, rows], QW.at[4 + e, rows], sib)

    relay_queries(1)
    relay_queries(3)
    project_q(1)
    project_q(3)
    ring_kx.pass_on()
    for e in (1, 3):
        cp_qn[e, 0].wait_recv()
        cp_qn[e, 1].wait_recv()
        project_q(4 + e)

    VT[HD:HD + 16, :] = jnp.ones((16, KEYS), BF)
    scale = math.log2(math.e) / math.sqrt(HD)

    def attend(base, size, before):
        q = Q[base:base + size, :]

        def scores(n):
            if n in before:
                before[n]()
            keys = slice(CHUNKS[n] * CH, (CHUNKS[n] + 1) * CH)
            if base == 0:
                VT[:HD, keys] = KV[keys, HD:].astype(F32).T.astype(BF)
            return dot_nt(KV[keys, :HD], q)

        m = None
        acc = None
        later = scores(0)
        for n in range(len(CHUNKS)):
            s = later
            if n + 1 < len(CHUNKS):
                later = scores(n + 1)
            top = jnp.max(s, axis=0, keepdims=True)
            new = top if m is None else jnp.maximum(m, top)
            p = jnp.exp2((s - new) * scale).astype(BF)
            pv = dot(VT[:, CHUNKS[n] * CH:(CHUNKS[n] + 1) * CH], p)
            acc = pv if acc is None else acc * jnp.exp2((m - new) * scale) + pv
            m = new
        heads = (acc[:HD] / acc[HD:HD + 1]).T
        HDS[base:base + size, :] = (heads * GS[base:base + size, :]).astype(BF)

    half = iota((48, 1), 0) < CAP

    def gather_heads(b):
        for p in range(8):
            h = HDS[place(p, b):place(p, b) + 48, :].astype(F32)
            both = jnp.concatenate([jnp.where(half, h, 0.0), jnp.where(half, 0.0, h)], axis=1)
            H[b, :, p * 256:(p + 1) * 256] = dot_tn(
                S[b, p * 48:(p + 1) * 48, :], both.astype(BF)
            ).astype(BF)

    def project_out(b, j):
        return dot(H[b], OW[j].reshape(2 * D, WC))

    cp_back, cp_via = {}, {}
    halves = (pl.ds(0, TOK // 2), pl.ds(TOK // 2, TOK // 2))
    ends = (dev(dx=3), dev(dx=1))

    def give_far(j):
        PS[j, 2] = project_out(2, j).astype(BF)
        for k in (0, 1):
            cp_via[j, k] = send(PS.at[j, 2, halves[1 - k]], TB.at[j, k], ends[k])

    def give_half(j, k, h):
        cp_back[j, k, h] = send(PS.at[j, k, halves[h]], RB.at[j, k, halves[h]], ends[k])

    def give_near(j, k):
        part = project_out(1 + 2 * k, j)
        late, n = 1 - k, TOK // 2
        PS[j, k, k * n:(k + 1) * n, :] = part[k * n:(k + 1) * n, :].astype(BF)
        PF[j, k] = part[late * n:(late + 1) * n, :]
        give_half(j, k, k)

    def finish(j):
        for k in (0, 1):
            late, n = 1 - k, TOK // 2
            cp_via[j, k].wait_recv()
            PS[j, k, late * n:(late + 1) * n, :] = (PF[j, k] + TB[j, k].astype(F32)).astype(BF)
            give_half(j, k, late)

    def give_all(j):
        have_weights(j)
        give_far(j)
        give_near(j, 0)
        give_near(j, 1)

    attend(0, 2 * SLOTS, {
        1: lambda: sib_keys(0),
        2: lambda: column_keys(1),
        3: lambda: column_keys(3),
        4: lambda: (sib_keys(1), relay_queries(2)),
        5: lambda: sib_keys(3),
        6: lambda: (column_keys(2), pass_weights(0)),
        7: lambda: sib_keys(2),
    })
    project_q(2)
    cp_qn[2, 0].wait_recv()
    cp_qn[2, 1].wait_recv()
    project_q(6)
    attend(2 * SLOTS, SLOTS, {
        1: lambda: pass_weights(1),
        6: lambda: relay_weights(0),
    })
    for d in (2, 1, 3):
        gather_heads(d)
    give_all(0)
    attend(3 * SLOTS, SLOTS, {
        1: lambda: pass_weights(2),
        3: lambda: (relay_weights(1), pass_weights(3)),
        5: lambda: give_all(1),
        7: lambda: (finish(0), relay_weights(2)),
    })
    gather_heads(0)
    own = {}
    give_all(2)
    relay_weights(3)
    own[0] = project_out(0, 0)
    finish(1)
    own[1] = project_out(0, 1)
    give_all(3)
    own[2] = project_out(0, 2)
    own[3] = project_out(0, 3)
    finish(2)
    finish(3)
    for j in range(NC):
        total = own[j]
        for k in (0, 1):
            cp_back[j, k, 0].wait_recv()
            cp_back[j, k, 1].wait_recv()
            total = total + RB[j, k].astype(F32)
        out[:, j * WC:(j + 1) * WC] = total.astype(BF)
    for cp in started:
        cp.wait_send()


def on_device(frames, kv_weight, query_weight, out_weight, expert_ids, gate_values):
    vmem, hbm = pl.BlockSpec(memory_space=pltpu.VMEM), pl.BlockSpec(memory_space=pltpu.HBM)
    return pl.pallas_call(
        kernel,
        out_shape=pltpu.VMEM((TOK, D), BF),
        in_specs=[hbm] * 6,
        out_specs=vmem,
        scratch_shapes=[
            pltpu.VMEM((4, TOK, D), BF),
            pltpu.VMEM((4, 8, TOK), F32),
            pltpu.VMEM((KEYS, 2 * HD), BF),
            pltpu.VMEM((8, 2 * D, HD), BF),
            pltpu.VMEM((NC, 8, 2 * HD, WC), BF),
            pltpu.VMEM((8, TOK, D), BF),
            pltpu.VMEM((4 * SLOTS, HD), BF),
            pltpu.VMEM((HD + 16, KEYS), BF),
            pltpu.VMEM((4 * SLOTS, HD), BF),
            pltpu.VMEM((4, TOK, 2 * D), BF),
            pltpu.VMEM((4, SLOTS, TOK), BF),
            pltpu.VMEM((4 * SLOTS, HD), F32),
            pltpu.VMEM((NC, 3, TOK, WC), BF),
            pltpu.VMEM((NC, 2, TOK // 2, WC), F32),
            pltpu.VMEM((NC, 2, TOK // 2, WC), BF),
            pltpu.VMEM((NC, 2, TOK, WC), BF),
            pltpu.VMEM((2 * HD, D), BF),
            pltpu.VMEM((D, 2 * HD), BF),
            pltpu.VMEM((4, TOK), jnp.int32),
            pltpu.VMEM((4, TOK), F32),
            pltpu.SemaphoreType.DMA((N_SEM,)),
            pltpu.SemaphoreType.DMA((N_SEM,)),
            pltpu.SemaphoreType.DMA((6,)),
        ],
        compiler_params=pltpu.CompilerParams(
            collective_id=0, has_side_effects=True, vmem_limit_bytes=56 << 20
        ),
        cost_estimate=pl.CostEstimate(
            flops=8_000_000_000, bytes_accessed=4_000_000, transcendentals=9_500_000
        ),
        name="moh",
    )(
        frames,
        kv_weight,
        query_weight.reshape(2 * D, HD),
        out_weight.reshape(2 * HD, D),
        expert_ids.T,
        gate_values.T,
    )


def solution(mesh):
    placed = (
        P(("seg", "tm"), None),
        P(),
        P("tm", None, None),
        P("tm", None, None),
        P(("seg", "tm"), None),
        P(("seg", "tm"), None),
    )
    return jax.shard_map(
        on_device, mesh=mesh, in_specs=placed, out_specs=P(("seg", "tm"), None), check_vma=False
    )
```

```python
import functools
import math

import jax
import jax.numpy as jnp
from jax import lax
from jax.experimental import pallas as pl
from jax.experimental.pallas import tpu as pltpu
from jax.sharding import PartitionSpec as P

MESH = pl.DeviceIdType.MESH
TOK = 192
D = 1024
HD = 128
CAP = 24
NEXP = 16
SLOTS = NEXP * CAP
KEYS = 6144
N_SEM = 128
CUTS = (0, 512, 768, 1024)
WIDTHS = (512, 256, 256)
NC = len(WIDTHS)
RANK = (0, 2, 6, 4, 1, 3, 7, 5)
CHUNKS = (0, 4, 1, 3, 5, 7, 2, 6)
CH = 768
BF = jnp.bfloat16
F32 = jnp.float32


def dot(a, b):
    return jnp.dot(a, b, preferred_element_type=F32)


def dot_nt(a, b):
    return lax.dot_general(a, b, (((1,), (1,)), ((), ())), preferred_element_type=F32)


def dot_tn(a, b, precision=None):
    return lax.dot_general(
        a, b, (((0,), (0,)), ((), ())), preferred_element_type=F32, precision=precision
    )


def place(p, b):
    return RANK[p] * 144 + (b - 1) * 48 if b else 1152 + RANK[p] * 48


def iota(shape, dim):
    return lax.broadcasted_iota(jnp.int32, shape, dim)


def kernel(
    frames_in, kvw_in, qw_in, ow_in, ids_in, gates_in, out,
    F, R, KV, QW, OW, X, Q, VT, HDS, H, S, GS, PS, PF, TB, RB, OWN, kvw, ids, gates, send_sem, recv_sem, keep_sem,
):
    z = lax.axis_index("seg")
    t = lax.axis_index("tm")
    c = lax.rem(t, 2)
    x = lax.rem(t // 2, 4)
    y = t // 8

    def dev(dx=0, dy=0, dc=0):
        yy = lax.rem(y + dy, 4)
        xx = lax.rem(x + dx, 4)
        return (z, (yy * 4 + xx) * 2 + lax.rem(c + dc, 2))

    sib = dev(dc=1)
    partners = [dev(dx=d) for d in (1, 2, 3)] + [dev(dy=d) for d in (1, 2, 3)] + [sib]
    frames, qw, ow = F.at[0], QW.at[0], OWN
    kept = [
        pltpu.make_async_copy(src, dst, keep_sem.at[n])
        for n, (src, dst) in enumerate((
            (frames_in, frames), (kvw_in, kvw), (ids_in, ids), (gates_in, gates), (qw_in, qw), (ow_in, ow),
        ))
    ]
    for cp in kept:
        cp.start()
    barrier = pltpu.get_barrier_semaphore()
    for p in partners:
        pl.semaphore_signal(barrier, inc=1, device_id=p, device_id_type=MESH)
    pl.semaphore_wait(barrier, len(partners))

    for cp in kept:
        cp.wait()
    started = []

    def send(src, dst, target):
        n = len(started)
        cp = pltpu.make_async_remote_copy(
            src_ref=src, dst_ref=dst, send_sem=send_sem.at[n], recv_sem=recv_sem.at[n],
            device_id=target, device_id_type=MESH,
        )
        cp.start()
        started.append(cp)
        return cp

    class Ring:
        def __init__(self, axis, own, slot, size):
            self.up, self.down = dev(**{axis: 1}), dev(**{axis: 3})
            self.slot, h = slot, size // 2
            self.a, self.b = pl.ds(0, h), pl.ds(h, h)
            a, b = own.at[self.a], own.at[self.b]
            self.a1 = send(a, slot(1).at[self.a], self.up)
            self.b3 = send(b, slot(3).at[self.b], self.down)
            self.b1 = send(b, slot(1).at[self.b], self.up)
            self.a3 = send(a, slot(3).at[self.a], self.down)

        def pass_on(self):
            self.a1.wait_recv()
            self.a2 = send(self.slot(1).at[self.a], self.slot(2).at[self.a], self.up)
            self.b3.wait_recv()
            self.b2 = send(self.slot(3).at[self.b], self.slot(2).at[self.b], self.down)

        def wait(self, d):
            for cp in {1: (self.b1,), 3: (self.a3,), 2: (self.a2, self.b2)}[d]:
                cp.wait_recv()

    def kv_at(d, e=0, n=1, sibling=False):
        return KV.at[pl.ds((16 * sibling + d * 4 + e) * TOK, n * TOK)]

    cp_ks = {}

    def kv_to_sib(*block):
        cp_ks[block] = send(kv_at(*block), kv_at(*block, sibling=True), sib)

    def key_values(d):
        KV[d * 4 * TOK:(d * 4 + 1) * TOK, :] = dot(F[d], kvw[...]).astype(BF)
        kv_to_sib(d)

    order = (1, 3, 2)
    def query_ring(j):
        rows = pl.ds(j * D, D)
        return Ring("dy", qw.at[rows], lambda e: QW.at[e, rows], D)

    ring_f = Ring("dx", frames, lambda d: F.at[d], TOK)
    R[0, 0:4] = ids[...].astype(F32)
    R[0, 4:8] = gates[...]
    cp_r = {d: send(R.at[0], R.at[d], dev(dx=d)) for d in order}
    key_values(0)
    ring_k = Ring("dy", kv_at(0), lambda e: kv_at(0, e), TOK)
    ring_q = [query_ring(0)]
    cp_qs = [send(qw, QW.at[4], sib)]
    for j in range(NC):
        OW[j][0] = ow[:, CUTS[j]:CUTS[j + 1]]

    i16 = iota((NEXP, 1), 0)
    owner = i16 >> 1
    oc = (c + (owner >> 2)) & 1
    oy = (y - (owner & 3)) & 3
    eid = (((oy * 4 + x) * 2 + oc) * 2 + (i16 & 1)).astype(F32)
    ej, ee = iota((SLOTS, NEXP), 0), iota((SLOTS, NEXP), 1) * CAP
    expand = (ej >= ee) & (ej < ee + CAP)
    e_rows = expand.astype(F32).astype(BF)
    i_col = jnp.sum(jnp.where(expand, ej - ee, 0).astype(F32), axis=1, keepdims=True)
    earlier = (iota((TOK, TOK), 0) < iota((TOK, TOK), 1)).astype(F32).astype(BF)

    def select(d):
        r = R[d]
        hit = jnp.zeros((NEXP, TOK), F32)
        gate = jnp.zeros((NEXP, TOK), F32)
        for k in range(4):
            same = r[k:k + 1, :] == eid
            hit = hit + same.astype(F32)
            gate = gate + jnp.where(same, r[4 + k:5 + k, :], 0.0)
        pos = dot(hit.astype(BF), earlier)
        posm = jnp.where(hit > 0.0, pos, -1.0)
        one_hot = (dot(e_rows, posm.astype(BF)) == i_col).astype(F32)
        S[d] = one_hot.astype(BF)
        gate_rows = jnp.dot(
            e_rows.astype(F32), gate, preferred_element_type=F32, precision=lax.Precision.HIGHEST
        )
        gate_col = jnp.broadcast_to(
            jnp.sum(one_hot * gate_rows, axis=1, keepdims=True), (SLOTS, HD)
        )
        picked = dot(S[d], F[d]).astype(BF)
        for p in range(8):
            X[p, d * 48:(d + 1) * 48, :] = picked[p * 48:(p + 1) * 48, :]
            GS[place(p, d):place(p, d) + 48, :] = gate_col[p * 48:(p + 1) * 48, :]

    select(0)

    ring_k.pass_on()
    ring_q.append(query_ring(1))
    ring_f.pass_on()
    ring_q[0].pass_on()
    for d in (1, 3):
        ring_f.wait(d)
        key_values(d)
        cp_r[d].wait_recv()
        select(d)
    for e in order:
        ring_k.wait(e)
    ring_kx = Ring("dx", kv_at(0, 1, 3), lambda d: kv_at(d, 1, 3), 3 * TOK)
    kv_to_sib(0, 1, 3)
    ring_q[1].pass_on()
    ring_o, cp_os = {}, {}

    def out_weights(j):
        cols = pl.ds(CUTS[j], WIDTHS[j])
        ring_o[j] = Ring("dy", ow.at[:, cols], lambda e: OW[j].at[e], 2 * HD)
        cp_os[j] = [send(OW[j].at[0], OW[j].at[4], sib)]

    def pass_weights(j):
        ring_o[j].pass_on()

    def relay_weights(j):
        for e in order:
            ring_o[j].wait(e)
            cp_os[j].append(send(OW[j].at[e], OW[j].at[4 + e], sib))

    def have_weights(j):
        for cp in cp_os[j]:
            cp.wait_recv()

    out_weights(0)
    ring_f.wait(2)
    key_values(2)
    cp_r[2].wait_recv()
    select(2)

    row = iota((TOK, 1), 0)
    first = jnp.zeros((TOK, 1), jnp.bool_)
    for b in range(4):
        first = first | ((row >= b * 48) & (row < b * 48 + CAP))

    def project_q(p):
        w = jnp.concatenate([QW[p, 0:D, :], QW[p, D:2 * D, :]], axis=1)
        both = dot(X[p], w)
        q = jnp.where(first, both[:, :HD], both[:, HD:]).astype(BF)
        Q[place(p, 0):place(p, 0) + 48, :] = q[:48, :]
        Q[place(p, 1):place(p, 1) + 144, :] = q[48:, :]

    project_q(0)
    cp_qs[0].wait_recv()
    project_q(4)

    cp_qn = {}

    def sib_keys(d):
        cp_ks[(d,)].wait_recv()
        cp_ks[d, 1, 3].wait_recv()

    def column_keys(d):
        ring_kx.wait(d)
        kv_to_sib(d, 1, 3)

    def relay_queries(e):
        for j in range(2):
            ring_q[j].wait(e)
            rows = pl.ds(j * D, D)
            cp_qn[e, j] = send(QW.at[e, rows], QW.at[4 + e, rows], sib)

    relay_queries(1)
    relay_queries(3)
    project_q(1)
    project_q(3)
    ring_kx.pass_on()
    for e in (1, 3):
        cp_qn[e, 0].wait_recv()
        cp_qn[e, 1].wait_recv()
        project_q(4 + e)

    VT[HD:HD + 16, :] = jnp.ones((16, KEYS), BF)
    scale = math.log2(math.e) / math.sqrt(HD)

    def attend(base, size, before):
        q = Q[base:base + size, :]

        def scores(n):
            if n in before:
                before[n]()
            keys = slice(CHUNKS[n] * CH, (CHUNKS[n] + 1) * CH)
            if base == 0:
                VT[:HD, keys] = KV[keys, HD:].astype(F32).T.astype(BF)
            return dot_nt(KV[keys, :HD], q)

        m = None
        acc = None
        later = scores(0)
        for n in range(len(CHUNKS)):
            s = later
            if n + 1 < len(CHUNKS):
                later = scores(n + 1)
            top = jnp.max(s, axis=0, keepdims=True)
            new = top if m is None else jnp.maximum(m, top)
            p = jnp.exp2((s - new) * scale).astype(BF)
            pv = dot(VT[:, CHUNKS[n] * CH:(CHUNKS[n] + 1) * CH], p)
            acc = pv if acc is None else acc * jnp.exp2((m - new) * scale) + pv
            m = new
        heads = (acc[:HD] / acc[HD:HD + 1]).T
        HDS[base:base + size, :] = (heads * GS[base:base + size, :]).astype(BF)

    half = iota((48, 1), 0) < CAP

    def gather_heads(b):
        for p in range(8):
            h = HDS[place(p, b):place(p, b) + 48, :].astype(F32)
            both = jnp.concatenate([jnp.where(half, h, 0.0), jnp.where(half, 0.0, h)], axis=1)
            H[b, :, p * 256:(p + 1) * 256] = dot_tn(
                S[b, p * 48:(p + 1) * 48, :], both.astype(BF)
            ).astype(BF)

    def project_out(b, j):
        return dot(H[b], OW[j][...].reshape(2 * D, WIDTHS[j]))

    cp_back, cp_via = {}, {}
    halves = (pl.ds(0, TOK // 2), pl.ds(TOK // 2, TOK // 2))
    ends = (dev(dx=3), dev(dx=1))

    def give_far(j):
        PS[j][2] = project_out(2, j).astype(BF)
        for k in (0, 1):
            cp_via[j, k] = send(PS[j].at[2, halves[1 - k]], TB[j].at[k], ends[k])

    def give_half(j, k, h):
        cp_back[j, k, h] = send(PS[j].at[k, halves[h]], RB[j].at[k, halves[h]], ends[k])

    def give_near(j, k):
        part = project_out(1 + 2 * k, j)
        late, n = 1 - k, TOK // 2
        PS[j][k, k * n:(k + 1) * n, :] = part[k * n:(k + 1) * n, :].astype(BF)
        PF[j][k] = part[late * n:(late + 1) * n, :]
        give_half(j, k, k)

    def finish(j):
        for k in (0, 1):
            late, n = 1 - k, TOK // 2
            cp_via[j, k].wait_recv()
            PS[j][k, late * n:(late + 1) * n, :] = (PF[j][k] + TB[j][k].astype(F32)).astype(BF)
            give_half(j, k, late)

    def give_all(j):
        have_weights(j)
        give_far(j)
        give_near(j, 0)
        give_near(j, 1)

    attend(0, 2 * SLOTS, {
        1: lambda: sib_keys(0),
        2: lambda: column_keys(1),
        3: lambda: column_keys(3),
        4: lambda: (sib_keys(1), relay_queries(2)),
        5: lambda: sib_keys(3),
        6: lambda: column_keys(2),
        7: lambda: (sib_keys(2), pass_weights(0), out_weights(1), out_weights(2)),
    })
    project_q(2)
    cp_qn[2, 0].wait_recv()
    cp_qn[2, 1].wait_recv()
    project_q(6)
    attend(2 * SLOTS, SLOTS, {
        7: lambda: relay_weights(0),
    })
    for d in (2, 1, 3):
        gather_heads(d)
    give_all(0)
    attend(3 * SLOTS, SLOTS, {
        2: lambda: pass_weights(1),
        6: lambda: pass_weights(2),
    })
    gather_heads(0)
    finish(0)
    relay_weights(1)
    own = {0: project_out(0, 0)}
    have_weights(1)
    give_far(1)
    relay_weights(2)
    give_near(1, 0)
    give_near(1, 1)
    have_weights(2)
    give_far(2)
    give_near(2, 0)
    give_near(2, 1)
    own[1] = project_out(0, 1)
    own[2] = project_out(0, 2)
    finish(1)
    finish(2)
    for j in range(NC):
        total = own[j]
        for k in (0, 1):
            cp_back[j, k, 0].wait_recv()
            cp_back[j, k, 1].wait_recv()
            total = total + RB[j][k].astype(F32)
        out[:, CUTS[j]:CUTS[j + 1]] = total.astype(BF)
    for cp in started:
        cp.wait_send()


def on_device(frames, kv_weight, query_weight, out_weight, expert_ids, gate_values):
    vmem, hbm = pl.BlockSpec(memory_space=pltpu.VMEM), pl.BlockSpec(memory_space=pltpu.HBM)
    return pl.pallas_call(
        kernel,
        out_shape=pltpu.VMEM((TOK, D), BF),
        in_specs=[hbm] * 6,
        out_specs=vmem,
        scratch_shapes=[
            pltpu.VMEM((4, TOK, D), BF),
            pltpu.VMEM((4, 8, TOK), F32),
            pltpu.VMEM((KEYS, 2 * HD), BF),
            pltpu.VMEM((8, 2 * D, HD), BF),
            [pltpu.VMEM((8, 2 * HD, w), BF) for w in WIDTHS],
            pltpu.VMEM((8, TOK, D), BF),
            pltpu.VMEM((4 * SLOTS, HD), BF),
            pltpu.VMEM((HD + 16, KEYS), BF),
            pltpu.VMEM((4 * SLOTS, HD), BF),
            pltpu.VMEM((4, TOK, 2 * D), BF),
            pltpu.VMEM((4, SLOTS, TOK), BF),
            pltpu.VMEM((4 * SLOTS, HD), F32),
            [pltpu.VMEM((3, TOK, w), BF) for w in WIDTHS],
            [pltpu.VMEM((2, TOK // 2, w), F32) for w in WIDTHS],
            [pltpu.VMEM((2, TOK // 2, w), BF) for w in WIDTHS],
            [pltpu.VMEM((2, TOK, w), BF) for w in WIDTHS],
            pltpu.VMEM((2 * HD, D), BF),
            pltpu.VMEM((D, 2 * HD), BF),
            pltpu.VMEM((4, TOK), jnp.int32),
            pltpu.VMEM((4, TOK), F32),
            pltpu.SemaphoreType.DMA((N_SEM,)),
            pltpu.SemaphoreType.DMA((N_SEM,)),
            pltpu.SemaphoreType.DMA((6,)),
        ],
        compiler_params=pltpu.CompilerParams(
            collective_id=0, has_side_effects=True, vmem_limit_bytes=56 << 20
        ),
        cost_estimate=pl.CostEstimate(
            flops=8_000_000_000, bytes_accessed=4_000_000, transcendentals=9_500_000
        ),
        name="moh",
    )(
        frames,
        kv_weight,
        query_weight.reshape(2 * D, HD),
        out_weight.reshape(2 * HD, D),
        expert_ids.T,
        gate_values.T,
    )


def solution(mesh):
    placed = (
        P(("seg", "tm"), None),
        P(),
        P("tm", None, None),
        P("tm", None, None),
        P(("seg", "tm"), None),
        P(("seg", "tm"), None),
    )
    return jax.shard_map(
        on_device, mesh=mesh, in_specs=placed, out_specs=P(("seg", "tm"), None), check_vma=False
    )
```

```python
import functools
import math

import jax
import jax.numpy as jnp
from jax import lax
from jax.experimental import pallas as pl
from jax.experimental.pallas import tpu as pltpu
from jax.sharding import PartitionSpec as P

MESH = pl.DeviceIdType.MESH
TOK = 192
D = 1024
HD = 128
CAP = 24
NEXP = 16
SLOTS = NEXP * CAP
KEYS = 6144
N_SEM = 128
CUTS = (0, 512, 768, 1024)
WIDTHS = (512, 256, 256)
NC = len(WIDTHS)
RANK = (0, 2, 6, 4, 1, 3, 7, 5)
CHUNKS = (0, 4, 1, 3, 5, 7, 2, 6)
CH = 768
BF = jnp.bfloat16
F32 = jnp.float32


def dot(a, b):
    return jnp.dot(a, b, preferred_element_type=F32)


def dot_nt(a, b):
    return lax.dot_general(a, b, (((1,), (1,)), ((), ())), preferred_element_type=F32)


def dot_tn(a, b, precision=None):
    return lax.dot_general(
        a, b, (((0,), (0,)), ((), ())), preferred_element_type=F32, precision=precision
    )


def place(p, b):
    return RANK[p] * 144 + (b - 1) * 48 if b else 1152 + RANK[p] * 48


def iota(shape, dim):
    return lax.broadcasted_iota(jnp.int32, shape, dim)


def kernel(
    frames_in, kvw_in, qw_in, ow_in, ids_in, gates_in, out,
    F, R, KV, QW, OW, X, Q, VT, HDS, H, S, GS, PS, PF, TB, RB, OWN, kvw, ids, gates, send_sem, recv_sem, keep_sem,
):
    z = lax.axis_index("seg")
    t = lax.axis_index("tm")
    c = lax.rem(t, 2)
    x = lax.rem(t // 2, 4)
    y = t // 8

    def dev(dx=0, dy=0, dc=0):
        yy = lax.rem(y + dy, 4)
        xx = lax.rem(x + dx, 4)
        return (z, (yy * 4 + xx) * 2 + lax.rem(c + dc, 2))

    sib = dev(dc=1)
    partners = [dev(dx=d) for d in (1, 2, 3)] + [dev(dy=d) for d in (1, 2, 3)] + [sib]
    frames, qw, ow = F.at[0], QW.at[0], OWN
    kept = [
        pltpu.make_async_copy(src, dst, keep_sem.at[n])
        for n, (src, dst) in enumerate((
            (frames_in, frames), (kvw_in, kvw), (ids_in, ids), (gates_in, gates), (qw_in, qw), (ow_in, ow),
        ))
    ]
    for cp in kept:
        cp.start()
    barrier = pltpu.get_barrier_semaphore()
    for p in partners:
        pl.semaphore_signal(barrier, inc=1, device_id=p, device_id_type=MESH)
    pl.semaphore_wait(barrier, len(partners))

    started = []

    def send(src, dst, target):
        n = len(started)
        cp = pltpu.make_async_remote_copy(
            src_ref=src, dst_ref=dst, send_sem=send_sem.at[n], recv_sem=recv_sem.at[n],
            device_id=target, device_id_type=MESH,
        )
        cp.start()
        started.append(cp)
        return cp

    class Ring:
        def __init__(self, axis, own, slot, size):
            self.up, self.down = dev(**{axis: 1}), dev(**{axis: 3})
            self.slot, h = slot, size // 2
            self.a, self.b = pl.ds(0, h), pl.ds(h, h)
            a, b = own.at[self.a], own.at[self.b]
            self.a1 = send(a, slot(1).at[self.a], self.up)
            self.b3 = send(b, slot(3).at[self.b], self.down)
            self.b1 = send(b, slot(1).at[self.b], self.up)
            self.a3 = send(a, slot(3).at[self.a], self.down)

        def pass_on(self):
            self.a1.wait_recv()
            self.a2 = send(self.slot(1).at[self.a], self.slot(2).at[self.a], self.up)
            self.b3.wait_recv()
            self.b2 = send(self.slot(3).at[self.b], self.slot(2).at[self.b], self.down)

        def wait(self, d):
            for cp in {1: (self.b1,), 3: (self.a3,), 2: (self.a2, self.b2)}[d]:
                cp.wait_recv()

    def kv_at(d, e=0, n=1, sibling=False):
        return KV.at[pl.ds((16 * sibling + d * 4 + e) * TOK, n * TOK)]

    cp_ks = {}

    def kv_to_sib(*block):
        cp_ks[block] = send(kv_at(*block), kv_at(*block, sibling=True), sib)

    def key_values(d):
        KV[d * 4 * TOK:(d * 4 + 1) * TOK, :] = dot(F[d], kvw[...]).astype(BF)
        kv_to_sib(d)

    order = (1, 3, 2)
    def query_ring(j):
        rows = pl.ds(j * D, D)
        return Ring("dy", qw.at[rows], lambda e: QW.at[e, rows], D)

    kept[0].wait()
    ring_f = Ring("dx", frames, lambda d: F.at[d], TOK)
    kept[2].wait()
    kept[3].wait()
    R[0, 0:4] = ids[...].astype(F32)
    R[0, 4:8] = gates[...]
    cp_r = {d: send(R.at[0], R.at[d], dev(dx=d)) for d in order}
    kept[1].wait()
    key_values(0)
    ring_k = Ring("dy", kv_at(0), lambda e: kv_at(0, e), TOK)
    kept[4].wait()
    ring_q = [query_ring(0)]
    cp_qs = [send(qw, QW.at[4], sib)]
    kept[5].wait()
    for j in range(NC):
        OW[j][0] = ow[:, CUTS[j]:CUTS[j + 1]]

    i16 = iota((NEXP, 1), 0)
    owner = i16 >> 1
    oc = (c + (owner >> 2)) & 1
    oy = (y - (owner & 3)) & 3
    eid = (((oy * 4 + x) * 2 + oc) * 2 + (i16 & 1)).astype(F32)
    ej, ee = iota((SLOTS, NEXP), 0), iota((SLOTS, NEXP), 1) * CAP
    expand = (ej >= ee) & (ej < ee + CAP)
    e_rows = expand.astype(F32).astype(BF)
    i_col = jnp.sum(jnp.where(expand, ej - ee, 0).astype(F32), axis=1, keepdims=True)
    earlier = (iota((TOK, TOK), 0) < iota((TOK, TOK), 1)).astype(F32).astype(BF)

    def select(d):
        r = R[d]
        hit = jnp.zeros((NEXP, TOK), F32)
        gate = jnp.zeros((NEXP, TOK), F32)
        for k in range(4):
            same = r[k:k + 1, :] == eid
            hit = hit + same.astype(F32)
            gate = gate + jnp.where(same, r[4 + k:5 + k, :], 0.0)
        pos = dot(hit.astype(BF), earlier)
        posm = jnp.where(hit > 0.0, pos, -1.0)
        one_hot = (dot(e_rows, posm.astype(BF)) == i_col).astype(F32)
        S[d] = one_hot.astype(BF)
        gate_rows = jnp.dot(
            e_rows.astype(F32), gate, preferred_element_type=F32, precision=lax.Precision.HIGHEST
        )
        gate_col = jnp.broadcast_to(
            jnp.sum(one_hot * gate_rows, axis=1, keepdims=True), (SLOTS, HD)
        )
        picked = dot(S[d], F[d]).astype(BF)
        for p in range(8):
            X[p, d * 48:(d + 1) * 48, :] = picked[p * 48:(p + 1) * 48, :]
            GS[place(p, d):place(p, d) + 48, :] = gate_col[p * 48:(p + 1) * 48, :]

    select(0)

    ring_k.pass_on()
    ring_q.append(query_ring(1))
    ring_f.pass_on()
    ring_q[0].pass_on()
    for d in (1, 3):
        ring_f.wait(d)
        key_values(d)
        cp_r[d].wait_recv()
        select(d)
    for e in order:
        ring_k.wait(e)
    ring_kx = Ring("dx", kv_at(0, 1, 3), lambda d: kv_at(d, 1, 3), 3 * TOK)
    kv_to_sib(0, 1, 3)
    ring_q[1].pass_on()
    ring_o, cp_os = {}, {}

    def out_weights(j):
        cols = pl.ds(CUTS[j], WIDTHS[j])
        ring_o[j] = Ring("dy", ow.at[:, cols], lambda e: OW[j].at[e], 2 * HD)
        cp_os[j] = [send(OW[j].at[0], OW[j].at[4], sib)]

    def pass_weights(j):
        ring_o[j].pass_on()

    def relay_weights(j):
        for e in order:
            ring_o[j].wait(e)
            cp_os[j].append(send(OW[j].at[e], OW[j].at[4 + e], sib))

    def have_weights(j):
        for cp in cp_os[j]:
            cp.wait_recv()

    out_weights(0)
    ring_f.wait(2)
    key_values(2)
    cp_r[2].wait_recv()
    select(2)

    row = iota((TOK, 1), 0)
    first = jnp.zeros((TOK, 1), jnp.bool_)
    for b in range(4):
        first = first | ((row >= b * 48) & (row < b * 48 + CAP))

    def project_q(p):
        w = jnp.concatenate([QW[p, 0:D, :], QW[p, D:2 * D, :]], axis=1)
        both = dot(X[p], w)
        q = jnp.where(first, both[:, :HD], both[:, HD:]).astype(BF)
        Q[place(p, 0):place(p, 0) + 48, :] = q[:48, :]
        Q[place(p, 1):place(p, 1) + 144, :] = q[48:, :]

    project_q(0)
    cp_qs[0].wait_recv()
    project_q(4)

    cp_qn = {}

    def sib_keys(d):
        cp_ks[(d,)].wait_recv()
        cp_ks[d, 1, 3].wait_recv()

    def column_keys(d):
        ring_kx.wait(d)
        kv_to_sib(d, 1, 3)

    def relay_queries(e):
        for j in range(2):
            ring_q[j].wait(e)
            rows = pl.ds(j * D, D)
            cp_qn[e, j] = send(QW.at[e, rows], QW.at[4 + e, rows], sib)

    relay_queries(1)
    relay_queries(3)
    project_q(1)
    project_q(3)
    ring_kx.pass_on()
    for e in (1, 3):
        cp_qn[e, 0].wait_recv()
        cp_qn[e, 1].wait_recv()
        project_q(4 + e)

    VT[HD:HD + 16, :] = jnp.ones((16, KEYS), BF)
    scale = math.log2(math.e) / math.sqrt(HD)

    def attend(base, size, before):
        q = Q[base:base + size, :]

        def scores(n):
            if n in before:
                before[n]()
            keys = slice(CHUNKS[n] * CH, (CHUNKS[n] + 1) * CH)
            if base == 0:
                VT[:HD, keys] = KV[keys, HD:].astype(F32).T.astype(BF)
            return dot_nt(KV[keys, :HD], q)

        m = None
        acc = None
        later = scores(0)
        for n in range(len(CHUNKS)):
            s = later
            if n + 1 < len(CHUNKS):
                later = scores(n + 1)
            top = jnp.max(s, axis=0, keepdims=True)
            new = top if m is None else jnp.maximum(m, top)
            p = jnp.exp2((s - new) * scale).astype(BF)
            pv = dot(VT[:, CHUNKS[n] * CH:(CHUNKS[n] + 1) * CH], p)
            acc = pv if acc is None else acc * jnp.exp2((m - new) * scale) + pv
            m = new
        heads = (acc[:HD] / acc[HD:HD + 1]).T
        HDS[base:base + size, :] = (heads * GS[base:base + size, :]).astype(BF)

    half = iota((48, 1), 0) < CAP

    def gather_heads(b):
        for p in range(8):
            h = HDS[place(p, b):place(p, b) + 48, :].astype(F32)
            both = jnp.concatenate([jnp.where(half, h, 0.0), jnp.where(half, 0.0, h)], axis=1)
            H[b, :, p * 256:(p + 1) * 256] = dot_tn(
                S[b, p * 48:(p + 1) * 48, :], both.astype(BF)
            ).astype(BF)

    def project_out(b, j):
        return dot(H[b], OW[j][...].reshape(2 * D, WIDTHS[j]))

    cp_back, cp_via = {}, {}
    halves = (pl.ds(0, TOK // 2), pl.ds(TOK // 2, TOK // 2))
    ends = (dev(dx=3), dev(dx=1))

    def give_far(j):
        PS[j][2] = project_out(2, j).astype(BF)
        for k in (0, 1):
            cp_via[j, k] = send(PS[j].at[2, halves[1 - k]], TB[j].at[k], ends[k])

    def give_half(j, k, h):
        cp_back[j, k, h] = send(PS[j].at[k, halves[h]], RB[j].at[k, halves[h]], ends[k])

    def give_near(j, k):
        part = project_out(1 + 2 * k, j)
        late, n = 1 - k, TOK // 2
        PS[j][k, k * n:(k + 1) * n, :] = part[k * n:(k + 1) * n, :].astype(BF)
        PF[j][k] = part[late * n:(late + 1) * n, :]
        give_half(j, k, k)

    def finish(j):
        for k in (0, 1):
            late, n = 1 - k, TOK // 2
            cp_via[j, k].wait_recv()
            PS[j][k, late * n:(late + 1) * n, :] = (PF[j][k] + TB[j][k].astype(F32)).astype(BF)
            give_half(j, k, late)

    def give_all(j):
        have_weights(j)
        give_far(j)
        give_near(j, 0)
        give_near(j, 1)

    attend(0, 2 * SLOTS, {
        1: lambda: sib_keys(0),
        2: lambda: column_keys(1),
        3: lambda: column_keys(3),
        4: lambda: (sib_keys(1), relay_queries(2)),
        5: lambda: sib_keys(3),
        6: lambda: column_keys(2),
        7: lambda: (sib_keys(2), pass_weights(0), out_weights(1), out_weights(2)),
    })
    project_q(2)
    cp_qn[2, 0].wait_recv()
    cp_qn[2, 1].wait_recv()
    project_q(6)
    attend(2 * SLOTS, SLOTS, {
        7: lambda: relay_weights(0),
    })
    for d in (2, 1, 3):
        gather_heads(d)
    give_all(0)
    attend(3 * SLOTS, SLOTS, {
        2: lambda: pass_weights(1),
        6: lambda: pass_weights(2),
    })
    gather_heads(0)
    finish(0)
    relay_weights(1)
    own = {0: project_out(0, 0)}
    have_weights(1)
    give_far(1)
    relay_weights(2)
    give_near(1, 0)
    give_near(1, 1)
    have_weights(2)
    give_far(2)
    give_near(2, 0)
    give_near(2, 1)
    own[1] = project_out(0, 1)
    own[2] = project_out(0, 2)
    finish(1)
    finish(2)
    for j in range(NC):
        total = own[j]
        for k in (0, 1):
            cp_back[j, k, 0].wait_recv()
            cp_back[j, k, 1].wait_recv()
            total = total + RB[j][k].astype(F32)
        out[:, CUTS[j]:CUTS[j + 1]] = total.astype(BF)
    for cp in started:
        cp.wait_send()


def on_device(frames, kv_weight, query_weight, out_weight, expert_ids, gate_values):
    vmem, hbm = pl.BlockSpec(memory_space=pltpu.VMEM), pl.BlockSpec(memory_space=pltpu.HBM)
    return pl.pallas_call(
        kernel,
        out_shape=pltpu.VMEM((TOK, D), BF),
        in_specs=[hbm] * 6,
        out_specs=vmem,
        scratch_shapes=[
            pltpu.VMEM((4, TOK, D), BF),
            pltpu.VMEM((4, 8, TOK), F32),
            pltpu.VMEM((KEYS, 2 * HD), BF),
            pltpu.VMEM((8, 2 * D, HD), BF),
            [pltpu.VMEM((8, 2 * HD, w), BF) for w in WIDTHS],
            pltpu.VMEM((8, TOK, D), BF),
            pltpu.VMEM((4 * SLOTS, HD), BF),
            pltpu.VMEM((HD + 16, KEYS), BF),
            pltpu.VMEM((4 * SLOTS, HD), BF),
            pltpu.VMEM((4, TOK, 2 * D), BF),
            pltpu.VMEM((4, SLOTS, TOK), BF),
            pltpu.VMEM((4 * SLOTS, HD), F32),
            [pltpu.VMEM((3, TOK, w), BF) for w in WIDTHS],
            [pltpu.VMEM((2, TOK // 2, w), F32) for w in WIDTHS],
            [pltpu.VMEM((2, TOK // 2, w), BF) for w in WIDTHS],
            [pltpu.VMEM((2, TOK, w), BF) for w in WIDTHS],
            pltpu.VMEM((2 * HD, D), BF),
            pltpu.VMEM((D, 2 * HD), BF),
            pltpu.VMEM((4, TOK), jnp.int32),
            pltpu.VMEM((4, TOK), F32),
            pltpu.SemaphoreType.DMA((N_SEM,)),
            pltpu.SemaphoreType.DMA((N_SEM,)),
            pltpu.SemaphoreType.DMA((6,)),
        ],
        compiler_params=pltpu.CompilerParams(
            collective_id=0, has_side_effects=True, vmem_limit_bytes=56 << 20
        ),
        cost_estimate=pl.CostEstimate(
            flops=8_000_000_000, bytes_accessed=4_000_000, transcendentals=9_500_000
        ),
        name="moh",
    )(
        frames,
        kv_weight,
        query_weight.reshape(2 * D, HD),
        out_weight.reshape(2 * HD, D),
        expert_ids.T,
        gate_values.T,
    )


def solution(mesh):
    placed = (
        P(("seg", "tm"), None),
        P(),
        P("tm", None, None),
        P("tm", None, None),
        P(("seg", "tm"), None),
        P(("seg", "tm"), None),
    )
    return jax.shard_map(
        on_device, mesh=mesh, in_specs=placed, out_specs=P(("seg", "tm"), None), check_vma=False
    )
```
